512 devices in a mesh: tm: 16 (over y, core), tile: 32 (over z, x).
Axes of the slice: x: 4, y: 8, z: 8, core: 2. Of those that a mesh axis runs over, the one named last changes fastest.
Arguments:
- features: bfloat16 [32, 128, 96, 128], P('tm', 'tile'), may hold values from -6 to 6
- gain_one: float32 [96], replicated, may hold values from 0.1 to 1.9
- gain_two: float32 [96], replicated, may hold values from 0.1 to 1.9
- gain_head: float32 [96], replicated, may hold values from 0.1 to 1.9
- conv_one: bfloat16 [3, 3, 3, 96, 96], replicated, may hold values from -0.125 to 0.125
- conv_two: bfloat16 [3, 3, 3, 96, 96], replicated, may hold values from -0.125 to 0.125
- conv_head: bfloat16 [3, 3, 3, 3, 96], replicated, may hold values from -0.125 to 0.125
Outputs:
- decoded: float32 [32, 128, 3, 128], P('tm', 'tile')
The draws below stay inside these ranges and needn't reach their ends.
All inputs are finite; a program needn't handle non-finite values.
Results may differ from the reference program's by a relative error of at most 0.009.
Values may be sent and summed in bfloat16 or wider, within the bound.
A program may use at most 128 MiB of HBM per device.

```python
import jax
import jax.numpy as jnp
from jax import lax

C = 96
OUT = 3
W = 128
FRAMES = 32
ROWS = 128


def level_of(own_key, shape, cuts, least, top_value):
    def one(axis_at, blocks):
        steps = jax.random.uniform(jax.random.fold_in(jax.random.fold_in(own_key, 6), axis_at), (blocks,), jnp.float32, least / len(cuts), top_value / len(cuts))
        return jnp.repeat(jnp.exp(steps), shape[axis_at] // blocks).reshape((-1,) + (1,) * (len(shape) - axis_at - 1))

    gain = one(*cuts[0])
    for cut in cuts[1:]:
        gain = gain * one(*cut)
    return gain


def normal_values(stream_key, shape, deviation, reach, split=(), kind=jnp.bfloat16):
    loudness = level_of(stream_key, shape, split, -0.22, 0.18) if split else 1.0
    result = jax.random.normal(stream_key, shape, jnp.float32) * deviation * loudness
    return jnp.minimum(jnp.maximum(result, -reach), reach).astype(kind)


def setup_inputs(seed: int = 0) -> dict:
    key_of = jax.random.split(jax.random.key(seed), 8)
    features = normal_values(key_of[0], (FRAMES, ROWS, C, W), 1.0, 6.0, ((0, 16), (1, 32)))
    gain_one = jnp.clip(1.0 + 0.18 * jax.random.normal(key_of[1], (C,), jnp.float32), 0.1, 1.9)
    gain_two = jnp.clip(1.0 + 0.18 * jax.random.normal(key_of[2], (C,), jnp.float32), 0.1, 1.9)
    gain_head = jnp.clip(1.0 + 0.18 * jax.random.normal(key_of[3], (C,), jnp.float32), 0.1, 1.9)
    conv_one = normal_values(key_of[4], (3, 3, 3, C, C), (27 * C) ** -0.5, 0.125)
    conv_two = normal_values(key_of[5], (3, 3, 3, C, C), (27 * C) ** -0.5, 0.125)
    conv_head = normal_values(key_of[6], (3, 3, 3, OUT, C), (27 * C) ** -0.5, 0.125)
    return {"features": features, "gain_one": gain_one, "gain_two": gain_two, "gain_head": gain_head, "conv_one": conv_one, "conv_two": conv_two, "conv_head": conv_head}


def activate(values, gains):
    values = values.astype(jnp.float32)
    square = lax.optimization_barrier(jnp.mean(values * values, axis=2, keepdims=True))
    normed = values * lax.rsqrt(square + 1e-06) * gains.astype(jnp.float32)[:, None]
    return jax.nn.silu(normed).astype(jnp.bfloat16)

def conv_whole(values, kernel):
    padded = jnp.pad(values.astype(jnp.float32), ((2, 0), (1, 1), (0, 0), (1, 1)))
    weights = kernel.astype(jnp.float32)
    row_count = values.shape[1]
    columns = values.shape[3]

    def one_frame(index):
        slab = lax.dynamic_slice_in_dim(padded, index, 3, 0)
        summed = jnp.zeros((row_count, kernel.shape[3], columns), jnp.float32)
        for step_t in range(3):
            for step_h in range(3):
                for step_w in range(3):
                    summed = summed + jnp.einsum('oc,hcw->how', weights[step_t, step_h, step_w], slab[step_t, step_h:step_h + row_count, :, step_w:step_w + columns], precision=lax.Precision.HIGHEST)
        return summed
    return lax.map(one_frame, jnp.arange(values.shape[0], dtype=jnp.int32))

def reference(features, gain_one, gain_two, gain_head, conv_one, conv_two, conv_head):
    first = activate(features, gain_one)
    hidden = conv_whole(first, conv_one).astype(jnp.bfloat16)
    second = activate(hidden, gain_two)
    branch = conv_whole(second, conv_two)
    residual_sum = (features.astype(jnp.float32) + branch).astype(jnp.bfloat16)
    head_in = activate(residual_sum, gain_head)
    return conv_whole(head_in, conv_head)
```

```python
import functools

import jax
import jax.numpy as jnp
from jax import lax
from jax.experimental import pallas as pl
from jax.experimental.pallas import tpu as pltpu
from jax.sharding import PartitionSpec as P

MESH = pl.DeviceIdType.MESH
F32 = jnp.float32
BF16 = jnp.bfloat16


def act(values, gains):
    square = jnp.sum(values * values, axis=0, keepdims=True) * (1.0 / values.shape[0])
    half = values * lax.rsqrt(square + 1e-06) * (gains * 0.5)
    return (half * jnp.tanh(half) + half).astype(BF16)


def shifted_sum(left, middle, right, column):
    width = column.shape[1]
    from_left = jnp.where(column == 0, 0.0, pltpu.roll(left, 1, 1))
    from_right = jnp.where(column == width - 1, 0.0, pltpu.roll(right, width - 1, 1))
    return from_left + middle + from_right


def kernel(
    sizes,
    features_ref,
    gain_one_ref,
    gain_two_ref,
    gain_head_ref,
    conv_one_ref,
    conv_two_ref,
    conv_head_ref,
    out_ref,
    own,
    raw_one,
    raw_two,
    taps_one,
    taps_two,
    taps_head,
    ext_one,
    ext_two,
    part,
    from_time,
    from_side,
    load_sem,
    send_one,
    recv_one,
    send_two,
    recv_two,
    send_head,
    recv_head,
):
    times, tiles, rows, chans, width = sizes
    t, s = lax.axis_index("tm"), lax.axis_index("tile")
    older, newer = t > 0, t < times - 1
    above, below = s > 0, s < tiles - 1

    loads = [
        pltpu.make_async_copy(features_ref, own, load_sem.at[0]),
        pltpu.make_async_copy(conv_one_ref, raw_one, load_sem.at[1]),
        pltpu.make_async_copy(conv_two_ref, raw_two, load_sem.at[2]),
    ]
    for load in loads:
        load.start()

    senders = [
        (older & above, (-1, -1)),
        (older & below, (-1, 1)),
        (above, (0, -1)),
        (below, (0, 1)),
        (older, (-1, 0)),
    ]
    above_one, below_one, newer_one = (flag.astype(jnp.int32) for flag in (above, below, newer))
    receivers = above_one + below_one + newer_one * (1 + above_one + below_one)
    barrier = pltpu.get_barrier_semaphore()
    for there, (dt, ds) in senders:

        @pl.when(there)
        def _():
            pl.semaphore_signal(barrier, inc=1, device_id=(t + dt, s + ds), device_id_type=MESH)

    for ext in (ext_one, ext_two):

        @pl.when(jnp.logical_not(older))
        def _():
            ext[0:2] = jnp.zeros((2, (rows + 2) * chans, width), BF16)

        @pl.when(jnp.logical_not(above))
        def _():
            ext[:, 0:chans] = jnp.zeros((4, chans, width), BF16)

        @pl.when(jnp.logical_not(below))
        def _():
            ext[:, (rows + 1) * chans :] = jnp.zeros((4, chans, width), BF16)

    def spread(gain_ref):
        return jnp.transpose(jnp.broadcast_to(gain_ref[...], (width, chans)))

    gain_one, gain_two, gain_head = spread(gain_one_ref), spread(gain_two_ref), spread(gain_head_ref)
    column = lax.broadcasted_iota(jnp.int32, (chans, width), 1)

    loads[0].wait()
    for f in range(2):
        for r in range(rows):
            ext_one[2 + f, (r + 1) * chans : (r + 2) * chans] = act(own[f, r].astype(F32), gain_one)

    pl.semaphore_wait(barrier, receivers)

    def row(at, frames, count=1):
        return (pl.ds(frames, 2), pl.ds(at * chans, count * chans))

    def exchange(ext, send_sem, recv_sem):
        plan = [
            (newer & above, older & below, (1, -1), row(1, 2), row(rows + 1, 0)),
            (newer & below, older & above, (1, 1), row(rows, 2), row(0, 0)),
            (above, below, (0, -1), row(1, 2), row(rows + 1, 2)),
            (below, above, (0, 1), row(rows, 2), row(0, 2)),
        ] + [(newer, older, (1, 0), row(r + 1, 2), row(r + 1, 0)) for r in range(rows)]
        return [
            (
                to,
                came,
                pltpu.make_async_remote_copy(
                    src_ref=ext.at[source],
                    dst_ref=ext.at[target],
                    send_sem=send_sem.at[i],
                    recv_sem=recv_sem.at[i],
                    device_id=(t + dt, s + ds),
                    device_id_type=MESH,
                ),
            )
            for i, (to, came, (dt, ds), source, target) in enumerate(plan)
        ]

    def start(copies):
        for to, _, copy in copies:
            pl.when(to)(copy.start)

    def arrive(copies):
        for _, came, copy in copies:
            pl.when(came)(copy.wait_recv)

    def leave(copies):
        for to, _, copy in copies:
            pl.when(to)(copy.wait_send)

    first_copies = exchange(ext_one, send_one, recv_one)
    start(first_copies)

    loads[1].wait()
    for k in range(9):
        taps_one[:, k * chans : (k + 1) * chans] = raw_one[k]
    loads[2].wait()
    for k in range(9):
        taps_two[:, k * chans : (k + 1) * chans] = raw_two[k]
    taps_head[...] = jnp.zeros_like(taps_head)
    for c in range(3):
        for b in range(3):
            for target in range(4):
                for f in range(2):
                    a = f + 2 - target
                    if 0 <= a <= 2:
                        at = ((c * 3 + b) * 2 + target // 2) * 8 + (target % 2) * 4
                        taps_head[at : at + 3, f * chans : (f + 1) * chans] = conv_head_ref[a, b, c].astype(F32)
    head_weights = taps_head[...].astype(BF16)

    def conv_row(taps, ext, r):
        stacks = [
            jnp.concatenate([ext[f + a, r * chans : (r + 3) * chans] for a in range(3)], axis=0) for f in range(2)
        ]
        product = jnp.dot(taps[...], jnp.concatenate(stacks, axis=1), preferred_element_type=F32)
        return [
            shifted_sum(
                *[product[c * chans : (c + 1) * chans, f * width : (f + 1) * width] for c in range(3)], column
            )
            for f in range(2)
        ]

    arrive(first_copies)
    second_copies = exchange(ext_two, send_two, recv_two)
    sent_with = {0: (0, 2, 4), 1: (5,), 2: (6,), rows - 1: (1, 3, 7)}
    for r in (0, rows - 1, 1, 2):
        for f, hidden in enumerate(conv_row(taps_one, ext_one, r)):
            hidden = hidden.astype(BF16).astype(F32)
            ext_two[2 + f, (r + 1) * chans : (r + 2) * chans] = act(hidden, gain_two)
        start([second_copies[i] for i in sent_with[r]])

    arrive(second_copies)
    summed = {}
    lane = lax.broadcasted_iota(jnp.int32, (8, width), 1)
    for pair in range(rows // 2):
        inputs = []
        for r in (2 * pair, 2 * pair + 1):
            branch = conv_row(taps_two, ext_two, r)
            heads = []
            for f in range(2):
                total = (own[f, r].astype(F32) + branch[f]).astype(BF16).astype(F32)
                heads.append(act(total, gain_head))
            inputs.append(jnp.concatenate(heads, axis=0))
        product = jnp.dot(head_weights, jnp.concatenate(inputs, axis=1), preferred_element_type=F32)
        for i in range(2):
            for c in range(3):
                for b in range(3):
                    for late in range(2):
                        at = ((c * 3 + b) * 2 + late) * 8
                        piece = product[at : at + 8, i * width : (i + 1) * width]
                        key = (late, 2 * pair + i + 2 - b, c)
                        summed[key] = summed[key] + piece if key in summed else piece
    for late in range(2):
        for r in range(rows + 2):
            part[late, r] = shifted_sum(*[summed[late, r, c] for c in range(3)], lane)

    plan = [
        (newer & above, older & below, (1, -1), part.at[1, 0], from_side.at[0]),
        (newer & below, older & above, (1, 1), part.at[1, rows + 1], from_side.at[1]),
        (above, below, (0, -1), part.at[0, 0], from_side.at[2]),
        (below, above, (0, 1), part.at[0, rows + 1], from_side.at[3]),
        (newer, older, (1, 0), part.at[1, pl.ds(1, rows)], from_time),
    ]
    head_copies = [
        (
            to,
            came,
            pltpu.make_async_remote_copy(
                src_ref=source,
                dst_ref=target,
                send_sem=send_head.at[i],
                recv_sem=recv_head.at[i],
                device_id=(t + dt, s + ds),
                device_id_type=MESH,
            ),
        )
        for i, (to, came, (dt, ds), source, target) in enumerate(plan)
    ]
    start(head_copies)

    for i, (_, came, _) in enumerate(head_copies):

        @pl.when(jnp.logical_not(came))
        def _():
            if i < 4:
                from_side[i] = jnp.zeros((8, width), F32)
            else:
                from_time[...] = jnp.zeros((rows, 8, width), F32)

    arrive(head_copies)
    for r in range(rows):
        total = part[0, r + 1] + from_time[r]
        if r == rows - 1:
            total = total + from_side[0] + from_side[2]
        if r == 0:
            total = total + from_side[1] + from_side[3]
        for f in range(2):
            for o in range(3):
                out_ref[f, o, r : r + 1] = total[4 * f + o : 4 * f + o + 1]

    leave(first_copies)
    leave(second_copies)
    leave(head_copies)


def local(times, tiles, features, gain_one, gain_two, gain_head, conv_one, conv_two, conv_head):
    frames, rows, chans, width = features.shape
    anywhere = pl.BlockSpec(memory_space=pl.ANY)
    vmem = pl.BlockSpec(memory_space=pltpu.VMEM)
    ext = pltpu.VMEM((4, (rows + 2) * chans, width), BF16)
    raw = pltpu.VMEM((9, 3 * chans, chans), BF16)
    taps = pltpu.VMEM((3 * chans, 9 * chans), BF16)
    dma = pltpu.SemaphoreType.DMA
    decoded = pl.pallas_call(
        functools.partial(kernel, (times, tiles, rows, chans, width)),
        out_shape=jax.ShapeDtypeStruct((frames, 3, rows, width), F32),
        in_specs=[anywhere, vmem, vmem, vmem, anywhere, anywhere, vmem],
        out_specs=vmem,
        scratch_shapes=[
            pltpu.VMEM(features.shape, BF16),
            raw,
            raw,
            taps,
            taps,
            pltpu.VMEM((144, 2 * chans), F32),
            ext,
            ext,
            pltpu.VMEM((2, rows + 2, 8, width), F32),
            pltpu.VMEM((rows, 8, width), F32),
            pltpu.VMEM((4, 8, width), F32),
            dma((3,)),
            dma((8,)),
            dma((8,)),
            dma((8,)),
            dma((8,)),
            dma((5,)),
            dma((5,)),
        ],
        compiler_params=pltpu.CompilerParams(
            collective_id=0, has_side_effects=True, vmem_limit_bytes=48 * 1024 * 1024
        ),
        cost_estimate=pl.CostEstimate(flops=1_100_000_000, bytes_accessed=1_300_000, transcendentals=400_000),
        name="decode",
    )(
        features,
        gain_one.reshape(1, chans),
        gain_two.reshape(1, chans),
        gain_head.reshape(1, chans),
        conv_one.reshape(9, 3 * chans, chans),
        conv_two.reshape(9, 3 * chans, chans),
        conv_head,
    )
    return jnp.transpose(decoded, (0, 2, 1, 3))


def solution(mesh):
    placed = (P("tm", "tile", None, None), P(), P(), P(), P(), P(), P())
    return jax.shard_map(
        functools.partial(local, mesh.shape["tm"], mesh.shape["tile"]),
        mesh=mesh,
        in_specs=placed,
        out_specs=P("tm", "tile", None, None),
        check_vma=False,
    )
```

```python
import functools

import jax
import jax.numpy as jnp
from jax import lax
from jax.experimental import pallas as pl
from jax.experimental.pallas import tpu as pltpu
from jax.sharding import PartitionSpec as P

MESH = pl.DeviceIdType.MESH
F32 = jnp.float32
BF16 = jnp.bfloat16


def act(values, gains):
    square = jnp.sum(values * values, axis=0, keepdims=True) * (1.0 / values.shape[0])
    half = values * lax.rsqrt(square + 1e-06) * (gains * 0.5)
    return (half * jnp.tanh(half) + half).astype(BF16)


def shifted_sum(left, middle, right, column):
    width = column.shape[1]
    from_left = jnp.where(column == 0, 0.0, pltpu.roll(left, 1, 1))
    from_right = jnp.where(column == width - 1, 0.0, pltpu.roll(right, width - 1, 1))
    return from_left + middle + from_right


def kernel(
    sizes,
    features_ref,
    gain_one_hbm,
    gain_two_hbm,
    gain_head_hbm,
    conv_one_ref,
    conv_two_ref,
    conv_head_hbm,
    out_ref,
    own,
    gain_one_ref,
    gain_two_ref,
    gain_head_ref,
    conv_head_ref,
    raw_one,
    raw_two,
    taps_one,
    taps_two,
    taps_head,
    ext_one,
    ext_two,
    part,
    from_time,
    from_side,
    load_sem,
    send_one,
    recv_one,
    send_two,
    recv_two,
    send_head,
    recv_head,
):
    times, tiles, rows, chans, width = sizes
    t, s = lax.axis_index("tm"), lax.axis_index("tile")
    older, newer = t > 0, t < times - 1
    above, below = s > 0, s < tiles - 1

    senders = [
        (older & above, (-1, -1)),
        (older & below, (-1, 1)),
        (above, (0, -1)),
        (below, (0, 1)),
        (older, (-1, 0)),
    ]
    above_one, below_one, newer_one = (flag.astype(jnp.int32) for flag in (above, below, newer))
    receivers = above_one + below_one + newer_one * (1 + above_one + below_one)
    barrier = pltpu.get_barrier_semaphore()
    for there, (dt, ds) in senders:

        @pl.when(there)
        def _():
            pl.semaphore_signal(barrier, inc=1, device_id=(t + dt, s + ds), device_id_type=MESH)

    loads = [
        pltpu.make_async_copy(source, target, load_sem.at[i])
        for i, (source, target) in enumerate(
            (
                (features_ref, own),
                (gain_one_hbm, gain_one_ref),
                (gain_two_hbm, gain_two_ref),
                (gain_head_hbm, gain_head_ref),
                (conv_one_ref, raw_one),
                (conv_two_ref, raw_two),
                (conv_head_hbm, conv_head_ref),
            )
        )
    ]
    for load in loads:
        load.start()

    for ext in (ext_one, ext_two):

        @pl.when(jnp.logical_not(older))
        def _():
            ext[0:2] = jnp.zeros((2, (rows + 2) * chans, width), BF16)

        @pl.when(jnp.logical_not(above))
        def _():
            ext[:, 0:chans] = jnp.zeros((4, chans, width), BF16)

        @pl.when(jnp.logical_not(below))
        def _():
            ext[:, (rows + 1) * chans :] = jnp.zeros((4, chans, width), BF16)

    upwards = lax.rem(s, 4) < 2
    near, far = jnp.where(upwards, 1, -1), jnp.where(upwards, -1, 1)
    order = [jnp.where(upwards, rows - 1 - i, i) for i in range(rows)]
    turns = [0, rows - 1, *range(1, rows - 1)]

    def rows_at(at, count=1):
        return pl.ds(pl.multiple_of(at * chans, 32), count * chans)

    def spread(gain_ref):
        return jnp.transpose(jnp.broadcast_to(gain_ref[...], (width, chans)))

    def exists(side):
        return jnp.where(side < 0, s > 0, s < tiles - 1)

    def remote(source, target, send_sem, recv_sem, device):
        return pltpu.make_async_remote_copy(
            src_ref=source,
            dst_ref=target,
            send_sem=send_sem,
            recv_sem=recv_sem,
            device_id=device,
            device_id_type=MESH,
        )

    def edge(ext, sems, side, later):
        source, target = jnp.where(side < 0, 1, rows), jnp.where(side < 0, rows + 1, 0)
        which = jnp.where(side < 0, 0, 1) + 2 * later
        return remote(
            ext.at[pl.ds(2, 2), rows_at(source)],
            ext.at[pl.ds(2 - 2 * later, 2), rows_at(target)],
            sems[0].at[which],
            sems[1].at[which],
            (t + later, s + side),
        )

    def onward(ext, sems, r):
        return remote(
            ext.at[pl.ds(2, 2), rows_at(r + 1)],
            ext.at[pl.ds(0, 2), rows_at(r + 1)],
            sems[0].at[4 + r],
            sems[1].at[4 + r],
            (t + 1, s),
        )

    odd = lax.rem(t, 2) == 1

    def send_both(copy, side):
        pl.when(newer & exists(side) & odd)(copy(side, 1).start)
        pl.when(exists(side))(copy(side, 0).start)
        pl.when(newer & exists(side) & jnp.logical_not(odd))(copy(side, 1).start)

    def send_edge(ext, sems, side):
        send_both(functools.partial(edge, ext, sems), side)

    def send_onward(ext, sems, r):
        pl.when(newer)(onward(ext, sems, r).start)

    def await_edge(ext, sems, side):
        pl.when(exists(side))(edge(ext, sems, -side, 0).wait_recv)
        pl.when(older & exists(side))(edge(ext, sems, -side, 1).wait_recv)

    def await_onward(ext, sems, r):
        pl.when(older)(onward(ext, sems, r).wait_recv)

    def await_row(ext, sems, i):
        if i == 0:
            await_onward(ext, sems, order[0])
            await_onward(ext, sems, order[1])
            await_edge(ext, sems, near)
        elif i == rows - 1:
            for r in order[2:]:
                await_onward(ext, sems, r)
            await_edge(ext, sems, far)

    def drain(ext, sems):
        for side in (near, far):
            pl.when(exists(side))(edge(ext, sems, side, 0).wait_send)
            pl.when(newer & exists(side))(edge(ext, sems, side, 1).wait_send)
        for r in order:
            pl.when(newer)(onward(ext, sems, r).wait_send)

    sems_one, sems_two = (send_one, recv_one), (send_two, recv_two)
    column = lax.broadcasted_iota(jnp.int32, (chans, width), 1)

    def first_act(r, gain):
        for f in range(2):
            ext_one[2 + f, rows_at(r + 1)] = act(own[f, r].astype(F32), gain)

    for load in loads[1:4]:
        load.wait()
    gain_one = spread(gain_one_ref)
    loads[0].wait()
    first_act(order[-1], gain_one)
    first_act(order[0], gain_one)
    pl.semaphore_wait(barrier, receivers)
    for side in (far, near):
        send_edge(ext_one, sems_one, side)
    send_onward(ext_one, sems_one, order[0])
    for i in range(1, rows):
        if i < rows - 1:
            first_act(order[i], gain_one)
        send_onward(ext_one, sems_one, order[i])
    gain_two, gain_head = spread(gain_two_ref), spread(gain_head_ref)

    loads[4].wait()
    for k in range(9):
        taps_one[:, k * chans : (k + 1) * chans] = raw_one[k]
    loads[5].wait()
    for k in range(9):
        taps_two[:, k * chans : (k + 1) * chans] = raw_two[k]
    loads[6].wait()
    taps_head[...] = jnp.zeros_like(taps_head)
    for b in range(3):
        step = jnp.where(upwards, 2 - b, b)
        for a in range(3):
            for c in range(3):
                piece = conv_head_ref[a, step, c].astype(F32)
                for f in range(2):
                    target = f + 2 - a
                    at = ((c * 3 + b) * 2 + target // 2) * 8 + (target % 2) * 4
                    taps_head[at : at + 3, f * chans : (f + 1) * chans] = piece
    head_weights = taps_head[...].astype(BF16)

    def conv_row(taps, ext, r):
        stacks = [jnp.concatenate([ext[f + a, rows_at(r, 3)] for a in range(3)], axis=0) for f in range(2)]
        product = jnp.dot(taps[...], jnp.concatenate(stacks, axis=1), preferred_element_type=F32)
        return [
            shifted_sum(
                *[product[c * chans : (c + 1) * chans, f * width : (f + 1) * width] for c in range(3)], column
            )
            for f in range(2)
        ]

    for i in turns:
        r = order[i]
        await_row(ext_one, sems_one, i)
        for f, hidden in enumerate(conv_row(taps_one, ext_one, r)):
            hidden = hidden.astype(BF16).astype(F32)
            ext_two[2 + f, rows_at(r + 1)] = act(hidden, gain_two)
        if i == 0:
            send_edge(ext_two, sems_two, near)
        if i == rows - 1:
            send_edge(ext_two, sems_two, far)
        send_onward(ext_two, sems_two, r)

    def head_edge(side, later):
        at = jnp.where(side == near, 0, rows + 1)
        which = jnp.where(side < 0, 0, 1) + 2 * later
        return remote(
            part.at[later, at], from_side.at[which], send_head.at[which], recv_head.at[which], (t + later, s + side)
        )

    head_onward = remote(part.at[1, pl.ds(1, rows)], from_time, send_head.at[4], recv_head.at[4], (t + 1, s))

    for side in (near, far):
        for later in range(2):
            sent = exists(side) & older if later else exists(side)

            @pl.when(jnp.logical_not(sent))
            def _():
                from_side[jnp.where(side < 0, 1, 0) + 2 * later] = jnp.zeros((8, width), F32)

    @pl.when(jnp.logical_not(older))
    def _():
        from_time[...] = jnp.zeros((rows, 8, width), F32)

    summed = {}
    lane = lax.broadcasted_iota(jnp.int32, (8, width), 1)

    def settle(place):
        for late in range(2):
            part[late, place] = shifted_sum(*[summed[late, place, c] for c in range(3)], lane)

    for i in turns:
        r = order[i]
        await_row(ext_two, sems_two, i)
        branch = conv_row(taps_two, ext_two, r)
        heads = []
        for f in range(2):
            total = (own[f, r].astype(F32) + branch[f]).astype(BF16).astype(F32)
            heads.append(act(total, gain_head))
        product = jnp.dot(head_weights, jnp.concatenate(heads, axis=0), preferred_element_type=F32)
        for c in range(3):
            for b in range(3):
                for late in range(2):
                    at = ((c * 3 + b) * 2 + late) * 8
                    piece = product[at : at + 8]
                    key = (late, i + 2 - b, c)
                    summed[key] = summed[key] + piece if key in summed else piece
        if i == 0:
            settle(0)
            send_both(head_edge, near)
        if i == rows - 1:
            settle(rows + 1)
            send_both(head_edge, far)
    for place in range(1, rows + 1):
        settle(place)
    pl.when(newer)(head_onward.start)

    drain(ext_one, sems_one)
    drain(ext_two, sems_two)
    pl.when(older)(head_onward.wait_recv)
    for i, r in enumerate(order):
        total = part[0, i + 1] + from_time[i]
        for at, side in ((0, near), (rows - 1, far)):
            if i == at:
                pl.when(exists(side))(head_edge(-side, 0).wait_recv)
                pl.when(older & exists(side))(head_edge(-side, 1).wait_recv)
                came = jnp.where(side < 0, 1, 0)
                total = total + from_side[came] + from_side[came + 2]
        for f in range(2):
            for o in range(3):
                out_ref[f, o, pl.ds(r, 1)] = total[4 * f + o : 4 * f + o + 1]

    for side in (near, far):
        pl.when(exists(side))(head_edge(side, 0).wait_send)
        pl.when(newer & exists(side))(head_edge(side, 1).wait_send)
    pl.when(newer)(head_onward.wait_send)


def local(times, tiles, features, gain_one, gain_two, gain_head, conv_one, conv_two, conv_head):
    frames, rows, chans, width = features.shape
    anywhere = pl.BlockSpec(memory_space=pl.ANY)
    vmem = pl.BlockSpec(memory_space=pltpu.VMEM)
    ext = pltpu.VMEM((4, (rows + 2) * chans, width), BF16)
    raw = pltpu.VMEM((9, 3 * chans, chans), BF16)
    taps = pltpu.VMEM((3 * chans, 9 * chans), BF16)
    dma = pltpu.SemaphoreType.DMA
    decoded = pl.pallas_call(
        functools.partial(kernel, (times, tiles, rows, chans, width)),
        out_shape=jax.ShapeDtypeStruct((frames, 3, rows, width), F32),
        in_specs=[anywhere] * 7,
        out_specs=vmem,
        scratch_shapes=[
            pltpu.VMEM(features.shape, BF16),
            pltpu.VMEM((1, chans), F32),
            pltpu.VMEM((1, chans), F32),
            pltpu.VMEM((1, chans), F32),
            pltpu.VMEM(conv_head.shape, BF16),
            raw,
            raw,
            taps,
            taps,
            pltpu.VMEM((144, 2 * chans), F32),
            ext,
            ext,
            pltpu.VMEM((2, rows + 2, 8, width), F32),
            pltpu.VMEM((rows, 8, width), F32),
            pltpu.VMEM((4, 8, width), F32),
            dma((7,)),
            dma((8,)),
            dma((8,)),
            dma((8,)),
            dma((8,)),
            dma((5,)),
            dma((5,)),
        ],
        compiler_params=pltpu.CompilerParams(
            collective_id=0, has_side_effects=True, vmem_limit_bytes=56524800
        ),
        cost_estimate=pl.CostEstimate(flops=1_100_000_000, bytes_accessed=1_300_000, transcendentals=400_000),
        name="decode",
    )(
        features,
        gain_one.reshape(1, chans),
        gain_two.reshape(1, chans),
        gain_head.reshape(1, chans),
        conv_one.reshape(9, 3 * chans, chans),
        conv_two.reshape(9, 3 * chans, chans),
        conv_head,
    )
    return jnp.transpose(decoded, (0, 2, 1, 3))


def solution(mesh):
    placed = (P("tm", "tile", None, None), P(), P(), P(), P(), P(), P())
    return jax.shard_map(
        functools.partial(local, mesh.shape["tm"], mesh.shape["tile"]),
        mesh=mesh,
        in_specs=placed,
        out_specs=P("tm", "tile", None, None),
        check_vma=False,
    )
```

```python
import functools

import jax
import jax.numpy as jnp
from jax import lax
from jax.experimental import pallas as pl
from jax.experimental.pallas import tpu as pltpu
from jax.sharding import PartitionSpec as P

MESH = pl.DeviceIdType.MESH
F32 = jnp.float32
BF16 = jnp.bfloat16


def act(values, gains):
    square = jnp.sum(values * values, axis=0, keepdims=True) * (1.0 / values.shape[0])
    half = values * lax.rsqrt(square + 1e-06) * (gains * 0.5)
    return (half * jnp.tanh(half) + half).astype(BF16)


def shifted_sum(left, middle, right, column):
    width = column.shape[1]
    from_left = jnp.where(column == 0, 0.0, pltpu.roll(left, 1, 1))
    from_right = jnp.where(column == width - 1, 0.0, pltpu.roll(right, width - 1, 1))
    return from_left + middle + from_right


def kernel(
    sizes,
    features_ref,
    gain_one_hbm,
    gain_two_hbm,
    gain_head_hbm,
    conv_one_ref,
    conv_two_ref,
    conv_head_hbm,
    out_ref,
    own,
    gain_one_ref,
    gain_two_ref,
    gain_head_ref,
    conv_head_ref,
    raw_one,
    raw_two,
    taps_one,
    taps_two,
    taps_head,
    ext_one,
    ext_two,
    part,
    from_time,
    from_side,
    load_sem,
    send_one,
    recv_one,
    send_two,
    recv_two,
    send_head,
    recv_head,
):
    times, tiles, rows, chans, width = sizes
    t, s = lax.axis_index("tm"), lax.axis_index("tile")
    older, newer = t > 0, t < times - 1
    above, below = s > 0, s < tiles - 1

    senders = [
        (older & above, (-1, -1)),
        (older & below, (-1, 1)),
        (above, (0, -1)),
        (below, (0, 1)),
        (older, (-1, 0)),
    ]
    above_one, below_one, newer_one = (flag.astype(jnp.int32) for flag in (above, below, newer))
    receivers = above_one + below_one + newer_one * (1 + above_one + below_one)
    barrier = pltpu.get_barrier_semaphore()
    for there, (dt, ds) in senders:

        @pl.when(there)
        def _():
            pl.semaphore_signal(barrier, inc=1, device_id=(t + dt, s + ds), device_id_type=MESH)

    loads = [
        pltpu.make_async_copy(source, target, load_sem.at[i])
        for i, (source, target) in enumerate(
            (
                (features_ref, own),
                (gain_one_hbm, gain_one_ref),
                (gain_two_hbm, gain_two_ref),
                (gain_head_hbm, gain_head_ref),
                (conv_one_ref, raw_one),
                (conv_two_ref, raw_two),
                (conv_head_hbm, conv_head_ref),
            )
        )
    ]
    for load in loads:
        load.start()

    for ext in (ext_one, ext_two):

        @pl.when(jnp.logical_not(older))
        def _():
            ext[0:2] = jnp.zeros((2, (rows + 2) * chans, width), BF16)

        @pl.when(jnp.logical_not(above))
        def _():
            ext[:, 0:chans] = jnp.zeros((4, chans, width), BF16)

        @pl.when(jnp.logical_not(below))
        def _():
            ext[:, (rows + 1) * chans :] = jnp.zeros((4, chans, width), BF16)

    upwards = lax.rem(s, 4) < 2
    near, far = jnp.where(upwards, 1, -1), jnp.where(upwards, -1, 1)
    order = [jnp.where(upwards, rows - 1 - i, i) for i in range(rows)]
    middle = list(range(1, rows - 1))

    outer = (lax.rem(s, 4) == 0) | (lax.rem(s, 4) == 3)
    lead = jnp.where(outer & (lax.rem(t, 2) == 0), far, near)
    lead_of_next = jnp.where(outer & (lax.rem(t, 2) == 1), far, near)

    def row_from(side, i):
        return jnp.where(side < 0, i, rows - 1 - i)


    def rows_at(at, count=1):
        return pl.ds(pl.multiple_of(at * chans, 32), count * chans)

    def spread(gain_ref):
        return jnp.transpose(jnp.broadcast_to(gain_ref[...], (width, chans)))

    def exists(side):
        return jnp.where(side < 0, s > 0, s < tiles - 1)

    def remote(source, target, send_sem, recv_sem, device):
        return pltpu.make_async_remote_copy(
            src_ref=source,
            dst_ref=target,
            send_sem=send_sem,
            recv_sem=recv_sem,
            device_id=device,
            device_id_type=MESH,
        )

    def edge(ext, sems, side, later):
        source, target = jnp.where(side < 0, 1, rows), jnp.where(side < 0, rows + 1, 0)
        which = jnp.where(side < 0, 0, 1) + 2 * later
        return remote(
            ext.at[pl.ds(2, 2), rows_at(source)],
            ext.at[pl.ds(2 - 2 * later, 2), rows_at(target)],
            sems[0].at[which],
            sems[1].at[which],
            (t + later, s + side),
        )

    def onward(ext, sems, r):
        return remote(
            ext.at[pl.ds(2, 2), rows_at(r + 1)],
            ext.at[pl.ds(0, 2), rows_at(r + 1)],
            sems[0].at[4 + r],
            sems[1].at[4 + r],
            (t + 1, s),
        )

    odd = lax.rem(t, 2) == 1

    def send_both(copy, side):
        pl.when(newer & exists(side) & odd)(copy(side, 1).start)
        pl.when(exists(side))(copy(side, 0).start)
        pl.when(newer & exists(side) & jnp.logical_not(odd))(copy(side, 1).start)

    def send_edge(ext, sems, side):
        send_both(functools.partial(edge, ext, sems), side)

    def send_onward(ext, sems, r):
        pl.when(newer)(onward(ext, sems, r).start)

    def await_edge(ext, sems, side):
        pl.when(exists(side))(edge(ext, sems, -side, 0).wait_recv)
        pl.when(older & exists(side))(edge(ext, sems, -side, 1).wait_recv)

    def await_onward(ext, sems, r):
        pl.when(older)(onward(ext, sems, r).wait_recv)

    def await_side(ext, sems, side):
        await_onward(ext, sems, row_from(side, 0))
        await_onward(ext, sems, row_from(side, 1))
        await_edge(ext, sems, side)

    def drain(ext, sems):
        for side in (near, far):
            pl.when(exists(side))(edge(ext, sems, side, 0).wait_send)
            pl.when(newer & exists(side))(edge(ext, sems, side, 1).wait_send)
        for r in order:
            pl.when(newer)(onward(ext, sems, r).wait_send)

    sems_one, sems_two = (send_one, recv_one), (send_two, recv_two)
    column = lax.broadcasted_iota(jnp.int32, (chans, width), 1)

    def first_act(r, gain):
        for f in range(2):
            ext_one[2 + f, rows_at(r + 1)] = act(own[f, r].astype(F32), gain)

    for load in loads[1:4]:
        load.wait()
    gain_one = spread(gain_one_ref)
    loads[0].wait()
    first_act(order[-1], gain_one)
    first_act(order[0], gain_one)
    pl.semaphore_wait(barrier, receivers)
    for side in (far, near):
        send_edge(ext_one, sems_one, side)
    for i in range(rows):
        r = row_from(lead_of_next, i)
        if 0 < i < rows - 1:
            first_act(r, gain_one)
        send_onward(ext_one, sems_one, r)
    gain_two, gain_head = spread(gain_two_ref), spread(gain_head_ref)

    loads[4].wait()
    for k in range(9):
        taps_one[:, k * chans : (k + 1) * chans] = raw_one[k]
    loads[5].wait()
    for k in range(9):
        taps_two[:, k * chans : (k + 1) * chans] = raw_two[k]
    loads[6].wait()
    taps_head[...] = jnp.zeros_like(taps_head)
    for b in range(3):
        step = jnp.where(upwards, 2 - b, b)
        for a in range(3):
            for c in range(3):
                piece = conv_head_ref[a, step, c].astype(F32)
                for f in range(2):
                    target = f + 2 - a
                    at = ((c * 3 + b) * 2 + target // 2) * 8 + (target % 2) * 4
                    taps_head[at : at + 3, f * chans : (f + 1) * chans] = piece
    head_weights = taps_head[...].astype(BF16)

    def conv_row(taps, ext, r):
        stacks = [jnp.concatenate([ext[f + a, rows_at(r, 3)] for a in range(3)], axis=0) for f in range(2)]
        product = jnp.dot(taps[...], jnp.concatenate(stacks, axis=1), preferred_element_type=F32)
        return [
            shifted_sum(
                *[product[c * chans : (c + 1) * chans, f * width : (f + 1) * width] for c in range(3)], column
            )
            for f in range(2)
        ]

    def second_act(r):
        for f, hidden in enumerate(conv_row(taps_one, ext_one, r)):
            hidden = hidden.astype(BF16).astype(F32)
            ext_two[2 + f, rows_at(r + 1)] = act(hidden, gain_two)

    for side in (lead, -lead):
        await_side(ext_one, sems_one, side)
        second_act(row_from(side, 0))
        send_edge(ext_two, sems_two, side)
        send_onward(ext_two, sems_two, row_from(side, 0))
    for i in middle:
        second_act(row_from(lead, i))
        send_onward(ext_two, sems_two, row_from(lead, i))

    def head_edge(side, later):
        at = jnp.where(side == near, 0, rows + 1)
        which = jnp.where(side < 0, 0, 1) + 2 * later
        return remote(
            part.at[later, at], from_side.at[which], send_head.at[which], recv_head.at[which], (t + later, s + side)
        )

    head_onward = remote(part.at[1, pl.ds(1, rows)], from_time, send_head.at[4], recv_head.at[4], (t + 1, s))

    for side in (near, far):
        for later in range(2):
            sent = exists(side) & older if later else exists(side)

            @pl.when(jnp.logical_not(sent))
            def _():
                from_side[jnp.where(side < 0, 1, 0) + 2 * later] = jnp.zeros((8, width), F32)

    @pl.when(jnp.logical_not(older))
    def _():
        from_time[...] = jnp.zeros((rows, 8, width), F32)

    summed = {}
    lane = lax.broadcasted_iota(jnp.int32, (8, width), 1)

    def settle(place):
        for late in range(2):
            part[late, place] = shifted_sum(*[summed[late, place, c] for c in range(3)], lane)

    for i in [0, rows - 1, *middle]:
        r = order[i]
        if i in (0, rows - 1):
            await_side(ext_two, sems_two, far if i else near)
        branch = conv_row(taps_two, ext_two, r)
        heads = []
        for f in range(2):
            total = (own[f, r].astype(F32) + branch[f]).astype(BF16).astype(F32)
            heads.append(act(total, gain_head))
        product = jnp.dot(head_weights, jnp.concatenate(heads, axis=0), preferred_element_type=F32)
        for c in range(3):
            for b in range(3):
                for late in range(2):
                    at = ((c * 3 + b) * 2 + late) * 8
                    piece = product[at : at + 8]
                    key = (late, i + 2 - b, c)
                    summed[key] = summed[key] + piece if key in summed else piece
        if i == 0:
            settle(0)
            send_both(head_edge, near)
        if i == rows - 1:
            settle(rows + 1)
            send_both(head_edge, far)
    for place in range(1, rows + 1):
        settle(place)
    pl.when(newer)(head_onward.start)

    drain(ext_one, sems_one)
    drain(ext_two, sems_two)
    pl.when(older)(head_onward.wait_recv)
    for i, r in enumerate(order):
        total = part[0, i + 1] + from_time[i]
        for at, side in ((0, near), (rows - 1, far)):
            if i == at:
                pl.when(exists(side))(head_edge(-side, 0).wait_recv)
                pl.when(older & exists(side))(head_edge(-side, 1).wait_recv)
                came = jnp.where(side < 0, 1, 0)
                total = total + from_side[came] + from_side[came + 2]
        for f in range(2):
            for o in range(3):
                out_ref[f, o, pl.ds(r, 1)] = total[4 * f + o : 4 * f + o + 1]

    for side in (near, far):
        pl.when(exists(side))(head_edge(side, 0).wait_send)
        pl.when(newer & exists(side))(head_edge(side, 1).wait_send)
    pl.when(newer)(head_onward.wait_send)


def local(times, tiles, features, gain_one, gain_two, gain_head, conv_one, conv_two, conv_head):
    frames, rows, chans, width = features.shape
    anywhere = pl.BlockSpec(memory_space=pl.ANY)
    vmem = pl.BlockSpec(memory_space=pltpu.VMEM)
    ext = pltpu.VMEM((4, (rows + 2) * chans, width), BF16)
    raw = pltpu.VMEM((9, 3 * chans, chans), BF16)
    taps = pltpu.VMEM((3 * chans, 9 * chans), BF16)
    dma = pltpu.SemaphoreType.DMA
    decoded = pl.pallas_call(
        functools.partial(kernel, (times, tiles, rows, chans, width)),
        out_shape=jax.ShapeDtypeStruct((frames, 3, rows, width), F32),
        in_specs=[anywhere] * 7,
        out_specs=vmem,
        scratch_shapes=[
            pltpu.VMEM(features.shape, BF16),
            pltpu.VMEM((1, chans), F32),
            pltpu.VMEM((1, chans), F32),
            pltpu.VMEM((1, chans), F32),
            pltpu.VMEM(conv_head.shape, BF16),
            raw,
            raw,
            taps,
            taps,
            pltpu.VMEM((144, 2 * chans), F32),
            ext,
            ext,
            pltpu.VMEM((2, rows + 2, 8, width), F32),
            pltpu.VMEM((rows, 8, width), F32),
            pltpu.VMEM((4, 8, width), F32),
            dma((7,)),
            dma((8,)),
            dma((8,)),
            dma((8,)),
            dma((8,)),
            dma((5,)),
            dma((5,)),
        ],
        compiler_params=pltpu.CompilerParams(
            collective_id=0, has_side_effects=True, vmem_limit_bytes=56524800
        ),
        cost_estimate=pl.CostEstimate(flops=1_100_000_000, bytes_accessed=1_300_000, transcendentals=400_000),
        name="decode",
    )(
        features,
        gain_one.reshape(1, chans),
        gain_two.reshape(1, chans),
        gain_head.reshape(1, chans),
        conv_one.reshape(9, 3 * chans, chans),
        conv_two.reshape(9, 3 * chans, chans),
        conv_head,
    )
    return jnp.transpose(decoded, (0, 2, 1, 3))


def solution(mesh):
    placed = (P("tm", "tile", None, None), P(), P(), P(), P(), P(), P())
    return jax.shard_map(
        functools.partial(local, mesh.shape["tm"], mesh.shape["tile"]),
        mesh=mesh,
        in_specs=placed,
        out_specs=P("tm", "tile", None, None),
        check_vma=False,
    )
```

```python
import functools

import jax
import jax.numpy as jnp
from jax import lax
from jax.experimental import pallas as pl
from jax.experimental.pallas import tpu as pltpu
from jax.sharding import PartitionSpec as P

MESH = pl.DeviceIdType.MESH
F32 = jnp.float32
BF16 = jnp.bfloat16


def act(values, gains):
    square = jnp.sum(values * values, axis=0, keepdims=True) * (1.0 / values.shape[0])
    half = values * lax.rsqrt(square + 1e-06) * (gains * 0.5)
    return (half * jnp.tanh(half) + half).astype(BF16)


def shifted_sum(left, middle, right, column):
    width = column.shape[1]
    from_left = jnp.where(column == 0, 0.0, pltpu.roll(left, 1, 1))
    from_right = jnp.where(column == width - 1, 0.0, pltpu.roll(right, width - 1, 1))
    return from_left + middle + from_right


def kernel(
    sizes,
    features_ref,
    gain_one_hbm,
    gain_two_hbm,
    gain_head_hbm,
    conv_one_ref,
    conv_two_ref,
    conv_head_hbm,
    out_ref,
    own,
    gain_one_ref,
    gain_two_ref,
    gain_head_ref,
    conv_head_ref,
    raw_one,
    raw_two,
    taps_one,
    taps_two,
    taps_head,
    ext_one,
    ext_two,
    part,
    from_time,
    from_side,
    load_sem,
    send_one,
    recv_one,
    send_two,
    recv_two,
    send_head,
    recv_head,
):
    times, tiles, rows, chans, width = sizes
    t, s = lax.axis_index("tm"), lax.axis_index("tile")
    older, newer = t > 0, t < times - 1
    above, below = s > 0, s < tiles - 1

    senders = [
        (older & above, (-1, -1)),
        (older & below, (-1, 1)),
        (above, (0, -1)),
        (below, (0, 1)),
        (older, (-1, 0)),
    ]
    above_one, below_one, newer_one = (flag.astype(jnp.int32) for flag in (above, below, newer))
    receivers = above_one + below_one + newer_one * (1 + above_one + below_one)
    barrier = pltpu.get_barrier_semaphore()
    for there, (dt, ds) in senders:

        @pl.when(there)
        def _():
            pl.semaphore_signal(barrier, inc=1, device_id=(t + dt, s + ds), device_id_type=MESH)

    loads = [
        pltpu.make_async_copy(source, target, load_sem.at[i])
        for i, (source, target) in enumerate(
            (
                (features_ref, own),
                (gain_one_hbm, gain_one_ref),
                (gain_two_hbm, gain_two_ref),
                (gain_head_hbm, gain_head_ref),
                (conv_one_ref, raw_one),
                (conv_two_ref, raw_two),
                (conv_head_hbm, conv_head_ref),
            )
        )
    ]
    for load in loads:
        load.start()

    for ext in (ext_one, ext_two):

        @pl.when(jnp.logical_not(older))
        def _():
            ext[0:2] = jnp.zeros((2, (rows + 2) * chans, width), BF16)

        @pl.when(jnp.logical_not(above))
        def _():
            ext[:, 0:chans] = jnp.zeros((4, chans, width), BF16)

        @pl.when(jnp.logical_not(below))
        def _():
            ext[:, (rows + 1) * chans :] = jnp.zeros((4, chans, width), BF16)

    upwards = lax.rem(s, 4) < 2
    near, far = jnp.where(upwards, 1, -1), jnp.where(upwards, -1, 1)
    order = [jnp.where(upwards, rows - 1 - i, i) for i in range(rows)]
    middle = list(range(1, rows - 1))

    outer = (lax.rem(s, 4) == 0) | (lax.rem(s, 4) == 3)
    lead = jnp.where(outer & (lax.rem(t, 2) == 0), far, near)
    lead_of_next = jnp.where(outer & (lax.rem(t, 2) == 1), far, near)

    def row_from(side, i):
        return jnp.where(side < 0, i, rows - 1 - i)


    def rows_at(at, count=1):
        return pl.ds(pl.multiple_of(at * chans, 32), count * chans)

    def spread(gain_ref):
        return jnp.transpose(jnp.broadcast_to(gain_ref[...], (width, chans)))

    def exists(side):
        return jnp.where(side < 0, s > 0, s < tiles - 1)

    def remote(source, target, send_sem, recv_sem, device):
        return pltpu.make_async_remote_copy(
            src_ref=source,
            dst_ref=target,
            send_sem=send_sem,
            recv_sem=recv_sem,
            device_id=device,
            device_id_type=MESH,
        )

    def edge(ext, sems, side, later):
        source, target = jnp.where(side < 0, 1, rows), jnp.where(side < 0, rows + 1, 0)
        which = jnp.where(side < 0, 0, 1) + 2 * later
        return remote(
            ext.at[pl.ds(2, 2), rows_at(source)],
            ext.at[pl.ds(2 - 2 * later, 2), rows_at(target)],
            sems[0].at[which],
            sems[1].at[which],
            (t + later, s + side),
        )

    def onward(ext, sems, r):
        return remote(
            ext.at[pl.ds(2, 2), rows_at(r + 1)],
            ext.at[pl.ds(0, 2), rows_at(r + 1)],
            sems[0].at[4 + r],
            sems[1].at[4 + r],
            (t + 1, s),
        )

    odd = lax.rem(t, 2) == 1

    def send_both(copy, side):
        pl.when(newer & exists(side) & odd)(copy(side, 1).start)
        pl.when(exists(side))(copy(side, 0).start)
        pl.when(newer & exists(side) & jnp.logical_not(odd))(copy(side, 1).start)

    def send_edge(ext, sems, side):
        send_both(functools.partial(edge, ext, sems), side)

    def send_onward(ext, sems, r):
        pl.when(newer)(onward(ext, sems, r).start)

    def await_edge(ext, sems, side):
        pl.when(exists(side))(edge(ext, sems, -side, 0).wait_recv)
        pl.when(older & exists(side))(edge(ext, sems, -side, 1).wait_recv)

    def await_onward(ext, sems, r):
        pl.when(older)(onward(ext, sems, r).wait_recv)

    def await_side(ext, sems, side):
        await_onward(ext, sems, row_from(side, 0))
        await_onward(ext, sems, row_from(side, 1))
        await_edge(ext, sems, side)

    def drain(ext, sems):
        for side in (near, far):
            pl.when(exists(side))(edge(ext, sems, side, 0).wait_send)
            pl.when(newer & exists(side))(edge(ext, sems, side, 1).wait_send)
        for r in order:
            pl.when(newer)(onward(ext, sems, r).wait_send)

    sems_one, sems_two = (send_one, recv_one), (send_two, recv_two)
    column = lax.broadcasted_iota(jnp.int32, (chans, width), 1)

    def first_act(r, gain):
        for f in range(2):
            ext_one[2 + f, rows_at(r + 1)] = act(own[f, r].astype(F32), gain)

    for load in loads[1:4]:
        load.wait()
    gain_one = spread(gain_one_ref)
    loads[0].wait()
    first_act(order[-1], gain_one)
    first_act(order[0], gain_one)
    pl.semaphore_wait(barrier, receivers)
    for side in (far, near):
        send_edge(ext_one, sems_one, side)
    for i in range(rows):
        r = row_from(lead_of_next, i)
        if 0 < i < rows - 1:
            first_act(r, gain_one)
        send_onward(ext_one, sems_one, r)
    gain_two, gain_head = spread(gain_two_ref), spread(gain_head_ref)

    loads[4].wait()
    for k in range(9):
        taps_one[:, k * chans : (k + 1) * chans] = raw_one[k]
    loads[5].wait()
    for k in range(9):
        taps_two[:, k * chans : (k + 1) * chans] = raw_two[k]
    loads[6].wait()
    taps_head[...] = jnp.zeros_like(taps_head)
    for b in range(3):
        step = jnp.where(upwards, 2 - b, b)
        for a in range(3):
            for c in range(3):
                piece = conv_head_ref[a, step, c].astype(F32)
                for f in range(2):
                    target = f + 2 - a
                    at = ((c * 3 + b) * 2 + target // 2) * 8 + (target % 2) * 4
                    taps_head[at : at + 3, f * chans : (f + 1) * chans] = piece
    head_weights = taps_head[...].astype(BF16)

    def conv_row(taps, ext, r):
        stacks = [jnp.concatenate([ext[f + a, rows_at(r, 3)] for a in range(3)], axis=0) for f in range(2)]
        product = jnp.dot(taps[...], jnp.concatenate(stacks, axis=1), preferred_element_type=F32)
        return [
            shifted_sum(
                *[product[c * chans : (c + 1) * chans, f * width : (f + 1) * width] for c in range(3)], column
            )
            for f in range(2)
        ]

    def second_act(r):
        for f, hidden in enumerate(conv_row(taps_one, ext_one, r)):
            hidden = hidden.astype(BF16).astype(F32)
            ext_two[2 + f, rows_at(r + 1)] = act(hidden, gain_two)

    for side in (lead, -lead):
        await_side(ext_one, sems_one, side)
        second_act(row_from(side, 0))
        send_edge(ext_two, sems_two, side)
        send_onward(ext_two, sems_two, row_from(side, 0))
    for i in middle:
        second_act(row_from(lead, i))
        send_onward(ext_two, sems_two, row_from(lead, i))

    def head_edge(side, later):
        at = jnp.where(side == near, 0, rows + 1)
        which = jnp.where(side < 0, 0, 1) + 2 * later
        return remote(
            part.at[later, at], from_side.at[which], send_head.at[which], recv_head.at[which], (t + later, s + side)
        )

    head_onward = remote(part.at[1, pl.ds(1, rows)], from_time, send_head.at[4], recv_head.at[4], (t + 1, s))

    for side in (near, far):
        for later in range(2):
            sent = exists(side) & older if later else exists(side)

            @pl.when(jnp.logical_not(sent))
            def _():
                from_side[jnp.where(side < 0, 1, 0) + 2 * later] = jnp.zeros((8, width), F32)

    @pl.when(jnp.logical_not(older))
    def _():
        from_time[...] = jnp.zeros((rows, 8, width), F32)

    summed = {}
    lane = lax.broadcasted_iota(jnp.int32, (8, width), 1)

    def settle(place):
        for late in range(2):
            part[late, place] = shifted_sum(*[summed[late, place, c] for c in range(3)], lane)

    for i in [0, rows - 1, *middle]:
        r = order[i]
        if i in (0, rows - 1):
            await_side(ext_two, sems_two, far if i else near)
        branch = conv_row(taps_two, ext_two, r)
        heads = []
        for f in range(2):
            total = (own[f, r].astype(F32) + branch[f]).astype(BF16).astype(F32)
            heads.append(act(total, gain_head))
        product = jnp.dot(head_weights, jnp.concatenate(heads, axis=0), preferred_element_type=F32)
        for c in range(3):
            for b in range(3):
                for late in range(2):
                    at = ((c * 3 + b) * 2 + late) * 8
                    piece = product[at : at + 8]
                    key = (late, i + 2 - b, c)
                    summed[key] = summed[key] + piece if key in summed else piece
        if i == 0:
            settle(0)
            send_both(head_edge, near)
        if i == rows - 1:
            settle(rows + 1)
            send_both(head_edge, far)
    for place in range(1, rows + 1):
        settle(place)
    pl.when(newer)(head_onward.start)

    drain(ext_one, sems_one)
    drain(ext_two, sems_two)
    pl.when(older)(head_onward.wait_recv)
    for i, r in enumerate(order):
        total = part[0, i + 1] + from_time[i]
        for at, side in ((0, near), (rows - 1, far)):
            if i == at:
                pl.when(exists(side))(head_edge(-side, 0).wait_recv)
                pl.when(older & exists(side))(head_edge(-side, 1).wait_recv)
                came = jnp.where(side < 0, 1, 0)
                total = total + from_side[came] + from_side[came + 2]
        for f in range(2):
            for o in range(3):
                out_ref[f, o, pl.ds(r, 1)] = total[4 * f + o : 4 * f + o + 1]

    for side in (near, far):
        pl.when(exists(side))(head_edge(side, 0).wait_send)
        pl.when(newer & exists(side))(head_edge(side, 1).wait_send)
    pl.when(newer)(head_onward.wait_send)


def local(times, tiles, features, gain_one, gain_two, gain_head, conv_one, conv_two, conv_head):
    frames, rows, chans, width = features.shape
    anywhere = pl.BlockSpec(memory_space=pl.ANY)
    vmem = pl.BlockSpec(memory_space=pltpu.VMEM)
    ext = pltpu.VMEM((4, (rows + 2) * chans, width), BF16)
    raw = pltpu.VMEM((9, 3 * chans, chans), BF16)
    taps = pltpu.VMEM((3 * chans, 9 * chans), BF16)
    dma = pltpu.SemaphoreType.DMA
    decoded = pl.pallas_call(
        functools.partial(kernel, (times, tiles, rows, chans, width)),
        out_shape=jax.ShapeDtypeStruct((frames, 3, rows, width), F32),
        in_specs=[anywhere] * 7,
        out_specs=vmem,
        scratch_shapes=[
            pltpu.VMEM(features.shape, BF16),
            pltpu.VMEM((1, chans), F32),
            pltpu.VMEM((1, chans), F32),
            pltpu.VMEM((1, chans), F32),
            pltpu.VMEM(conv_head.shape, BF16),
            raw,
            raw,
            taps,
            taps,
            pltpu.VMEM((144, 2 * chans), F32),
            ext,
            ext,
            pltpu.VMEM((2, rows + 2, 8, width), F32),
            pltpu.VMEM((rows, 8, width), F32),
            pltpu.VMEM((4, 8, width), F32),
            dma((7,)),
            dma((8,)),
            dma((8,)),
            dma((8,)),
            dma((8,)),
            dma((5,)),
            dma((5,)),
        ],
        compiler_params=pltpu.CompilerParams(
            collective_id=0, has_side_effects=True, vmem_limit_bytes=48 * 1024 * 1024
        ),
        cost_estimate=pl.CostEstimate(flops=1_100_000_000, bytes_accessed=1_300_000, transcendentals=400_000),
        name="decode",
    )(
        *(
            pltpu.with_memory_space_constraint(operand, pltpu.HBM)
            for operand in (
                features,
                gain_one.reshape(1, chans),
                gain_two.reshape(1, chans),
                gain_head.reshape(1, chans),
                conv_one.reshape(9, 3 * chans, chans),
                conv_two.reshape(9, 3 * chans, chans),
                conv_head,
            )
        )
    )
    return jnp.transpose(decoded, (0, 2, 1, 3))


def solution(mesh):
    placed = (P("tm", "tile", None, None), P(), P(), P(), P(), P(), P())
    return jax.shard_map(
        functools.partial(local, mesh.shape["tm"], mesh.shape["tile"]),
        mesh=mesh,
        in_specs=placed,
        out_specs=P("tm", "tile", None, None),
        check_vma=False,
    )
```

```python
import functools

import jax
import jax.numpy as jnp
from jax import lax
from jax.experimental import pallas as pl
from jax.experimental.pallas import tpu as pltpu
from jax.sharding import PartitionSpec as P

MESH = pl.DeviceIdType.MESH
F32 = jnp.float32
BF16 = jnp.bfloat16


def act(values, gains):
    square = jnp.sum(values * values, axis=0, keepdims=True) * (1.0 / values.shape[0])
    half = values * lax.rsqrt(square + 1e-06) * (gains * 0.5)
    return (half * jnp.tanh(half) + half).astype(BF16)


def shifted_sum(left, middle, right, column):
    width = column.shape[1]
    from_left = jnp.where(column == 0, 0.0, pltpu.roll(left, 1, 1))
    from_right = jnp.where(column == width - 1, 0.0, pltpu.roll(right, width - 1, 1))
    return from_left + middle + from_right


def kernel(
    sizes,
    features_ref,
    gain_one_hbm,
    gain_two_hbm,
    gain_head_hbm,
    conv_one_ref,
    conv_two_ref,
    conv_head_hbm,
    out_ref,
    own,
    gain_one_ref,
    gain_two_ref,
    gain_head_ref,
    conv_head_ref,
    raw_one,
    raw_two,
    taps_one,
    taps_two,
    taps_head,
    ext_one,
    ext_two,
    part,
    from_time,
    from_side,
    load_sem,
    send_one,
    recv_one,
    send_two,
    recv_two,
    send_head,
    recv_head,
    ready,
):
    times, tiles, rows, chans, width = sizes
    t, s = lax.axis_index("tm"), lax.axis_index("tile")
    older, newer = t > 0, t < times - 1
    above, below = s > 0, s < tiles - 1

    odd = lax.rem(t, 2) == 1
    even = jnp.logical_not(odd)
    lent = odd & newer & (t == times // 2 - 1)
    lent_to = even & older & (t == times // 2)

    senders = [
        (older & above & jnp.logical_not(lent_to), (-1, -1)),
        (lent & below, (1, 1)),
        (older & below, (-1, 1)),
        (above, (0, -1)),
        (below, (0, 1)),
        (older, (-1, 0)),
    ]
    above_one, below_one, newer_one, lent_one, lent_to_one = (
        flag.astype(jnp.int32) for flag in (above, below, newer, lent, lent_to)
    )
    receivers = above_one + below_one + newer_one * (1 + above_one + below_one)
    receivers = receivers - lent_one * below_one + lent_to_one * above_one
    barrier = pltpu.get_barrier_semaphore()
    for there, (dt, ds) in senders:

        @pl.when(there)
        def _():
            pl.semaphore_signal(barrier, inc=1, device_id=(t + dt, s + ds), device_id_type=MESH)

    loads = [
        pltpu.make_async_copy(source, target, load_sem.at[i])
        for i, (source, target) in enumerate(
            (
                (features_ref, own),
                (gain_one_hbm, gain_one_ref),
                (gain_two_hbm, gain_two_ref),
                (gain_head_hbm, gain_head_ref),
                (conv_one_ref, raw_one),
                (conv_two_ref, raw_two),
                (conv_head_hbm, conv_head_ref),
            )
        )
    ]
    for load in loads:
        load.start()

    for ext in (ext_one, ext_two):

        @pl.when(jnp.logical_not(older))
        def _():
            ext[0:2] = jnp.zeros((2, (rows + 2) * chans, width), BF16)

        @pl.when(jnp.logical_not(above))
        def _():
            ext[:, 0:chans] = jnp.zeros((4, chans, width), BF16)

        @pl.when(jnp.logical_not(below))
        def _():
            ext[:, (rows + 1) * chans :] = jnp.zeros((4, chans, width), BF16)

    upwards = lax.rem(s, 4) < 2
    near, far = jnp.where(upwards, 1, -1), jnp.where(upwards, -1, 1)
    order = [jnp.where(upwards, rows - 1 - i, i) for i in range(rows)]
    middle = list(range(1, rows - 1))

    outer = (lax.rem(s, 4) == 0) | (lax.rem(s, 4) == 3)
    lead = jnp.where(outer & (lax.rem(t, 2) == 0), far, near)
    lead_of_next = jnp.where(outer & (lax.rem(t, 2) == 1), far, near)

    def row_from(side, i):
        return jnp.where(side < 0, i, rows - 1 - i)


    def rows_at(at, count=1):
        return pl.ds(pl.multiple_of(at * chans, 32), count * chans)

    def spread(gain_ref):
        return jnp.transpose(jnp.broadcast_to(gain_ref[...], (width, chans)))

    def exists(side):
        return jnp.where(side < 0, s > 0, s < tiles - 1)

    def remote(source, target, send_sem, recv_sem, device):
        return pltpu.make_async_remote_copy(
            src_ref=source,
            dst_ref=target,
            send_sem=send_sem,
            recv_sem=recv_sem,
            device_id=device,
            device_id_type=MESH,
        )

    def edge(ext, sems, side, later):
        source, target = jnp.where(side < 0, 1, rows), jnp.where(side < 0, rows + 1, 0)
        which = jnp.where(side < 0, 0, 1) + 2 * later
        return remote(
            ext.at[pl.ds(2, 2), rows_at(source)],
            ext.at[pl.ds(2 - 2 * later, 2), rows_at(target)],
            sems[0].at[which],
            sems[1].at[which],
            (t + later, s + side),
        )

    def onward(ext, sems, r):
        return remote(
            ext.at[pl.ds(2, 2), rows_at(r + 1)],
            ext.at[pl.ds(0, 2), rows_at(r + 1)],
            sems[0].at[4 + r],
            sems[1].at[4 + r],
            (t + 1, s),
        )

    def handed_on():
        here = pl.ds(0, chans)
        return remote(
            ext_one.at[pl.ds(2, 2), here], ext_one.at[pl.ds(0, 2), here], send_one.at[3], recv_one.at[3], (t + 1, s)
        )

    def straight(ext, side):
        there = newer & exists(side)
        return there & jnp.logical_not(lent & (side > 0)) if ext is ext_one else there

    def send_both(copy, side, there):
        ahead = odd
        pl.when(there & ahead)(copy(side, 1).start)
        pl.when(exists(side))(copy(side, 0).start)
        pl.when(there & jnp.logical_not(ahead))(copy(side, 1).start)

    def send_edge(ext, sems, side):
        if ext is ext_two:

            @pl.when(lent & below & (side > 0))
            def _():
                pl.semaphore_wait(ready, 1)

        send_both(functools.partial(edge, ext, sems), side, straight(ext, side))

    def send_onward(ext, sems, r):
        pl.when(newer)(onward(ext, sems, r).start)

    def await_edge(ext, sems, side):
        early = lent & (side < 0) if ext is ext_one else t < 0
        pl.when(exists(side) & jnp.logical_not(early))(edge(ext, sems, -side, 0).wait_recv)
        pl.when(older & exists(side))(edge(ext, sems, -side, 1).wait_recv)

    def await_onward(ext, sems, r):
        pl.when(older)(onward(ext, sems, r).wait_recv)

    def await_side(ext, sems, side):
        await_onward(ext, sems, row_from(side, 0))
        await_onward(ext, sems, row_from(side, 1))
        await_edge(ext, sems, side)

    def drain(ext, sems):
        for side in (near, far):
            pl.when(exists(side))(edge(ext, sems, side, 0).wait_send)
            pl.when(straight(ext, side))(edge(ext, sems, side, 1).wait_send)
        for r in order:
            pl.when(newer)(onward(ext, sems, r).wait_send)

    sems_one, sems_two = (send_one, recv_one), (send_two, recv_two)
    column = lax.broadcasted_iota(jnp.int32, (chans, width), 1)

    def first_act(r, gain):
        for f in range(2):
            ext_one[2 + f, rows_at(r + 1)] = act(own[f, r].astype(F32), gain)

    for load in loads[1:4]:
        load.wait()
    gain_one = spread(gain_one_ref)
    loads[0].wait()
    first_act(order[-1], gain_one)
    first_act(order[0], gain_one)
    pl.semaphore_wait(barrier, receivers)

    @pl.when(lent_to & above)
    def _():
        pl.semaphore_signal(ready, inc=1, device_id=(t - 1, s - 1), device_id_type=MESH)

    for side in (far, near):
        send_edge(ext_one, sems_one, side)
    for i in range(rows):
        r = row_from(lead_of_next, i)
        if 0 < i < rows - 1:
            first_act(r, gain_one)
        send_onward(ext_one, sems_one, r)
    gain_two, gain_head = spread(gain_two_ref), spread(gain_head_ref)

    loads[4].wait()
    for k in range(9):
        taps_one[:, k * chans : (k + 1) * chans] = raw_one[k]
    loads[5].wait()
    for k in range(9):
        taps_two[:, k * chans : (k + 1) * chans] = raw_two[k]
    loads[6].wait()
    taps_head[...] = jnp.zeros_like(taps_head)
    for b in range(3):
        step = jnp.where(upwards, 2 - b, b)
        for a in range(3):
            for c in range(3):
                piece = conv_head_ref[a, step, c].astype(F32)
                for f in range(2):
                    target = f + 2 - a
                    at = ((c * 3 + b) * 2 + target // 2) * 8 + (target % 2) * 4
                    taps_head[at : at + 3, f * chans : (f + 1) * chans] = piece
    head_weights = taps_head[...].astype(BF16)

    @pl.when(lent & above)
    def _():
        edge(ext_one, sems_one, 1, 0).wait_recv()
        handed_on().start()

    def conv_row(taps, ext, r):
        stacks = [jnp.concatenate([ext[f + a, rows_at(r, 3)] for a in range(3)], axis=0) for f in range(2)]
        product = jnp.dot(taps[...], jnp.concatenate(stacks, axis=1), preferred_element_type=F32)
        return [
            shifted_sum(
                *[product[c * chans : (c + 1) * chans, f * width : (f + 1) * width] for c in range(3)], column
            )
            for f in range(2)
        ]

    def second_act(r):
        for f, hidden in enumerate(conv_row(taps_one, ext_one, r)):
            hidden = hidden.astype(BF16).astype(F32)
            ext_two[2 + f, rows_at(r + 1)] = act(hidden, gain_two)

    for side in (lead, -lead):
        await_side(ext_one, sems_one, side)
        second_act(row_from(side, 0))
        send_edge(ext_two, sems_two, side)
        send_onward(ext_two, sems_two, row_from(side, 0))
    for i in middle:
        second_act(row_from(lead, i))
        send_onward(ext_two, sems_two, row_from(lead, i))

    def head_edge(side, later):
        at = jnp.where(side == near, 0, rows + 1)
        which = jnp.where(side < 0, 0, 1) + 2 * later
        return remote(
            part.at[later, at], from_side.at[which], send_head.at[which], recv_head.at[which], (t + later, s + side)
        )

    head_onward = remote(part.at[1, pl.ds(1, rows)], from_time, send_head.at[4], recv_head.at[4], (t + 1, s))

    for side in (near, far):
        for later in range(2):
            sent = exists(side) & older if later else exists(side)

            @pl.when(jnp.logical_not(sent))
            def _():
                from_side[jnp.where(side < 0, 1, 0) + 2 * later] = jnp.zeros((8, width), F32)

    @pl.when(jnp.logical_not(older))
    def _():
        from_time[...] = jnp.zeros((rows, 8, width), F32)

    summed = {}
    lane = lax.broadcasted_iota(jnp.int32, (8, width), 1)

    def settle(place):
        for late in range(2):
            part[late, place] = shifted_sum(*[summed[late, place, c] for c in range(3)], lane)

    for i in [0, rows - 1, *middle]:
        r = order[i]
        if i in (0, rows - 1):
            await_side(ext_two, sems_two, far if i else near)
        branch = conv_row(taps_two, ext_two, r)
        heads = []
        for f in range(2):
            total = (own[f, r].astype(F32) + branch[f]).astype(BF16).astype(F32)
            heads.append(act(total, gain_head))
        product = jnp.dot(head_weights, jnp.concatenate(heads, axis=0), preferred_element_type=F32)
        for c in range(3):
            for b in range(3):
                for late in range(2):
                    at = ((c * 3 + b) * 2 + late) * 8
                    piece = product[at : at + 8]
                    key = (late, i + 2 - b, c)
                    summed[key] = summed[key] + piece if key in summed else piece
        if i == 0:
            settle(0)
            send_both(head_edge, near, newer & exists(near))
        if i == rows - 1:
            settle(rows + 1)
            send_both(head_edge, far, newer & exists(far))
    for place in range(1, rows + 1):
        settle(place)
    pl.when(newer)(head_onward.start)

    drain(ext_one, sems_one)
    pl.when(lent & above)(handed_on().wait_send)
    drain(ext_two, sems_two)
    pl.when(older)(head_onward.wait_recv)
    for i, r in enumerate(order):
        total = part[0, i + 1] + from_time[i]
        for at, side in ((0, near), (rows - 1, far)):
            if i == at:
                pl.when(exists(side))(head_edge(-side, 0).wait_recv)
                pl.when(older & exists(side))(head_edge(-side, 1).wait_recv)
                came = jnp.where(side < 0, 1, 0)
                total = total + from_side[came] + from_side[came + 2]
        for f in range(2):
            for o in range(3):
                out_ref[f, o, pl.ds(r, 1)] = total[4 * f + o : 4 * f + o + 1]

    for side in (near, far):
        pl.when(exists(side))(head_edge(side, 0).wait_send)
        pl.when(newer & exists(side))(head_edge(side, 1).wait_send)
    pl.when(newer)(head_onward.wait_send)


def local(times, tiles, features, gain_one, gain_two, gain_head, conv_one, conv_two, conv_head):
    frames, rows, chans, width = features.shape
    anywhere = pl.BlockSpec(memory_space=pl.ANY)
    vmem = pl.BlockSpec(memory_space=pltpu.VMEM)
    ext = pltpu.VMEM((4, (rows + 2) * chans, width), BF16)
    raw = pltpu.VMEM((9, 3 * chans, chans), BF16)
    taps = pltpu.VMEM((3 * chans, 9 * chans), BF16)
    dma = pltpu.SemaphoreType.DMA
    decoded = pl.pallas_call(
        functools.partial(kernel, (times, tiles, rows, chans, width)),
        out_shape=jax.ShapeDtypeStruct((frames, 3, rows, width), F32),
        in_specs=[anywhere] * 7,
        out_specs=vmem,
        scratch_shapes=[
            pltpu.VMEM(features.shape, BF16),
            pltpu.VMEM((1, chans), F32),
            pltpu.VMEM((1, chans), F32),
            pltpu.VMEM((1, chans), F32),
            pltpu.VMEM(conv_head.shape, BF16),
            raw,
            raw,
            taps,
            taps,
            pltpu.VMEM((144, 2 * chans), F32),
            ext,
            ext,
            pltpu.VMEM((2, rows + 2, 8, width), F32),
            pltpu.VMEM((rows, 8, width), F32),
            pltpu.VMEM((4, 8, width), F32),
            dma((7,)),
            dma((8,)),
            dma((8,)),
            dma((8,)),
            dma((8,)),
            dma((5,)),
            dma((5,)),
            pltpu.SemaphoreType.REGULAR,
        ],
        compiler_params=pltpu.CompilerParams(
            collective_id=0, has_side_effects=True, vmem_limit_bytes=48 * 1024 * 1024
        ),
        cost_estimate=pl.CostEstimate(flops=1_100_000_000, bytes_accessed=1_300_000, transcendentals=400_000),
        name="decode",
    )(
        *(
            pltpu.with_memory_space_constraint(operand, pltpu.HBM)
            for operand in (
                features,
                gain_one.reshape(1, chans),
                gain_two.reshape(1, chans),
                gain_head.reshape(1, chans),
                conv_one.reshape(9, 3 * chans, chans),
                conv_two.reshape(9, 3 * chans, chans),
                conv_head,
            )
        )
    )
    return jnp.transpose(decoded, (0, 2, 1, 3))


def solution(mesh):
    placed = (P("tm", "tile", None, None), P(), P(), P(), P(), P(), P())
    return jax.shard_map(
        functools.partial(local, mesh.shape["tm"], mesh.shape["tile"]),
        mesh=mesh,
        in_specs=placed,
        out_specs=P("tm", "tile", None, None),
        check_vma=False,
    )
```

```python
import functools

import jax
import jax.numpy as jnp
from jax import lax
from jax.experimental import pallas as pl
from jax.experimental.pallas import tpu as pltpu
from jax.sharding import PartitionSpec as P

MESH = pl.DeviceIdType.MESH
F32 = jnp.float32
BF16 = jnp.bfloat16


def act(values, gains):
    square = jnp.sum(values * values, axis=0, keepdims=True) * (1.0 / values.shape[0])
    half = values * lax.rsqrt(square + 1e-06) * (gains * 0.5)
    return (half * jnp.tanh(half) + half).astype(BF16)


def shifted_sum(left, middle, right, column):
    width = column.shape[1]
    from_left = jnp.where(column == 0, 0.0, pltpu.roll(left, 1, 1))
    from_right = jnp.where(column == width - 1, 0.0, pltpu.roll(right, width - 1, 1))
    return from_left + middle + from_right


def kernel(
    sizes,
    features_ref,
    gain_one_hbm,
    gain_two_hbm,
    gain_head_hbm,
    conv_one_ref,
    conv_two_ref,
    conv_head_hbm,
    out_ref,
    own,
    gain_one_ref,
    gain_two_ref,
    gain_head_ref,
    conv_head_ref,
    raw_one,
    raw_two,
    taps_one,
    taps_two,
    taps_head,
    ext_one,
    ext_two,
    part,
    from_time,
    from_side,
    load_sem,
    send_one,
    recv_one,
    send_two,
    recv_two,
    send_head,
    recv_head,
    ready,
):
    times, tiles, rows, chans, width = sizes
    t, s = lax.axis_index("tm"), lax.axis_index("tile")
    older, newer = t > 0, t < times - 1
    above, below = s > 0, s < tiles - 1

    odd = lax.rem(t, 2) == 1
    even = jnp.logical_not(odd)
    lent = odd & newer & (t < times // 2)
    lent_to = even & older & (t <= times // 2)

    senders = [
        (older & above & jnp.logical_not(lent_to), (-1, -1)),
        (lent & below, (1, 1)),
        (older & below, (-1, 1)),
        (above, (0, -1)),
        (below, (0, 1)),
        (older, (-1, 0)),
    ]
    above_one, below_one, newer_one, lent_one, lent_to_one = (
        flag.astype(jnp.int32) for flag in (above, below, newer, lent, lent_to)
    )
    receivers = above_one + below_one + newer_one * (1 + above_one + below_one)
    receivers = receivers - lent_one * below_one + lent_to_one * above_one
    barrier = pltpu.get_barrier_semaphore()
    for there, (dt, ds) in senders:

        @pl.when(there)
        def _():
            pl.semaphore_signal(barrier, inc=1, device_id=(t + dt, s + ds), device_id_type=MESH)

    loads = [
        pltpu.make_async_copy(source, target, load_sem.at[i])
        for i, (source, target) in enumerate(
            (
                (features_ref, own),
                (gain_one_hbm, gain_one_ref),
                (gain_two_hbm, gain_two_ref),
                (gain_head_hbm, gain_head_ref),
                (conv_one_ref, raw_one),
                (conv_two_ref, raw_two),
                (conv_head_hbm, conv_head_ref),
            )
        )
    ]
    for load in loads:
        load.start()

    for ext in (ext_one, ext_two):

        @pl.when(jnp.logical_not(older))
        def _():
            ext[0:2] = jnp.zeros((2, (rows + 2) * chans, width), BF16)

        @pl.when(jnp.logical_not(above))
        def _():
            ext[:, 0:chans] = jnp.zeros((4, chans, width), BF16)

        @pl.when(jnp.logical_not(below))
        def _():
            ext[:, (rows + 1) * chans :] = jnp.zeros((4, chans, width), BF16)

    upwards = lax.rem(s, 4) < 2
    near, far = jnp.where(upwards, 1, -1), jnp.where(upwards, -1, 1)
    order = [jnp.where(upwards, rows - 1 - i, i) for i in range(rows)]
    middle = list(range(1, rows - 1))

    outer = (lax.rem(s, 4) == 0) | (lax.rem(s, 4) == 3)
    lead = jnp.where(outer & (lax.rem(t, 2) == 0), far, near)
    lead_of_next = jnp.where(outer & (lax.rem(t, 2) == 1), far, near)

    def row_from(side, i):
        return jnp.where(side < 0, i, rows - 1 - i)


    def rows_at(at, count=1):
        return pl.ds(pl.multiple_of(at * chans, 32), count * chans)

    def spread(gain_ref):
        return jnp.transpose(jnp.broadcast_to(gain_ref[...], (width, chans)))

    def exists(side):
        return jnp.where(side < 0, s > 0, s < tiles - 1)

    def remote(source, target, send_sem, recv_sem, device):
        return pltpu.make_async_remote_copy(
            src_ref=source,
            dst_ref=target,
            send_sem=send_sem,
            recv_sem=recv_sem,
            device_id=device,
            device_id_type=MESH,
        )

    def edge(ext, sems, side, later):
        source, target = jnp.where(side < 0, 1, rows), jnp.where(side < 0, rows + 1, 0)
        which = jnp.where(side < 0, 0, 1) + 2 * later
        return remote(
            ext.at[pl.ds(2, 2), rows_at(source)],
            ext.at[pl.ds(2 - 2 * later, 2), rows_at(target)],
            sems[0].at[which],
            sems[1].at[which],
            (t + later, s + side),
        )

    def onward(ext, sems, r):
        return remote(
            ext.at[pl.ds(2, 2), rows_at(r + 1)],
            ext.at[pl.ds(0, 2), rows_at(r + 1)],
            sems[0].at[4 + r],
            sems[1].at[4 + r],
            (t + 1, s),
        )

    def handed_on():
        here = pl.ds(0, chans)
        return remote(
            ext_one.at[pl.ds(2, 2), here], ext_one.at[pl.ds(0, 2), here], send_one.at[3], recv_one.at[3], (t + 1, s)
        )

    def straight(ext, side):
        there = newer & exists(side)
        return there & jnp.logical_not(lent & (side > 0)) if ext is ext_one else there

    def send_both(copy, side, there, ahead=odd):
        pl.when(there & ahead)(copy(side, 1).start)
        pl.when(exists(side))(copy(side, 0).start)
        pl.when(there & jnp.logical_not(ahead))(copy(side, 1).start)

    def send_edge(ext, sems, side):
        if ext is ext_two:

            @pl.when(lent & below & (side > 0))
            def _():
                pl.semaphore_wait(ready, 1)

        ahead = odd | (t >= times // 2) if ext is ext_one else odd
        send_both(functools.partial(edge, ext, sems), side, straight(ext, side), ahead)

    def send_onward(ext, sems, r):
        pl.when(newer)(onward(ext, sems, r).start)

    def await_edge(ext, sems, side):
        early = lent & (side < 0) if ext is ext_one else t < 0
        pl.when(exists(side) & jnp.logical_not(early))(edge(ext, sems, -side, 0).wait_recv)
        pl.when(older & exists(side))(edge(ext, sems, -side, 1).wait_recv)

    def await_onward(ext, sems, r):
        pl.when(older)(onward(ext, sems, r).wait_recv)

    def await_side(ext, sems, side):
        await_onward(ext, sems, row_from(side, 0))
        await_onward(ext, sems, row_from(side, 1))
        await_edge(ext, sems, side)

    def drain(ext, sems):
        for side in (near, far):
            pl.when(exists(side))(edge(ext, sems, side, 0).wait_send)
            pl.when(straight(ext, side))(edge(ext, sems, side, 1).wait_send)
        for r in order:
            pl.when(newer)(onward(ext, sems, r).wait_send)

    sems_one, sems_two = (send_one, recv_one), (send_two, recv_two)
    column = lax.broadcasted_iota(jnp.int32, (chans, width), 1)

    def first_act(r, gain):
        for f in range(2):
            ext_one[2 + f, rows_at(r + 1)] = act(own[f, r].astype(F32), gain)

    for load in loads[1:4]:
        load.wait()
    gain_one = spread(gain_one_ref)
    loads[0].wait()
    first_act(order[-1], gain_one)
    first_act(order[0], gain_one)
    pl.semaphore_wait(barrier, receivers)

    @pl.when(lent_to & above)
    def _():
        pl.semaphore_signal(ready, inc=1, device_id=(t - 1, s - 1), device_id_type=MESH)

    for side in (far, near):
        send_edge(ext_one, sems_one, side)
    for i in range(rows):
        r = row_from(lead_of_next, i)
        if 0 < i < rows - 1:
            first_act(r, gain_one)
        send_onward(ext_one, sems_one, r)
    gain_two, gain_head = spread(gain_two_ref), spread(gain_head_ref)

    loads[4].wait()
    for k in range(9):
        taps_one[:, k * chans : (k + 1) * chans] = raw_one[k]
    loads[5].wait()
    for k in range(9):
        taps_two[:, k * chans : (k + 1) * chans] = raw_two[k]
    loads[6].wait()
    taps_head[...] = jnp.zeros_like(taps_head)
    for b in range(3):
        step = jnp.where(upwards, 2 - b, b)
        for a in range(3):
            for c in range(3):
                piece = conv_head_ref[a, step, c].astype(F32)
                for f in range(2):
                    target = f + 2 - a
                    at = ((c * 3 + b) * 2 + target // 2) * 8 + (target % 2) * 4
                    taps_head[at : at + 3, f * chans : (f + 1) * chans] = piece
    head_weights = taps_head[...].astype(BF16)

    @pl.when(lent & above)
    def _():
        edge(ext_one, sems_one, 1, 0).wait_recv()
        handed_on().start()

    def conv_row(taps, ext, r):
        stacks = [jnp.concatenate([ext[f + a, rows_at(r, 3)] for a in range(3)], axis=0) for f in range(2)]
        product = jnp.dot(taps[...], jnp.concatenate(stacks, axis=1), preferred_element_type=F32)
        return [
            shifted_sum(
                *[product[c * chans : (c + 1) * chans, f * width : (f + 1) * width] for c in range(3)], column
            )
            for f in range(2)
        ]

    def second_act(r):
        for f, hidden in enumerate(conv_row(taps_one, ext_one, r)):
            hidden = hidden.astype(BF16).astype(F32)
            ext_two[2 + f, rows_at(r + 1)] = act(hidden, gain_two)

    for side in (lead, -lead):
        await_side(ext_one, sems_one, side)
        second_act(row_from(side, 0))
        send_edge(ext_two, sems_two, side)
        send_onward(ext_two, sems_two, row_from(side, 0))
    for i in middle:
        second_act(row_from(lead, i))
        send_onward(ext_two, sems_two, row_from(lead, i))

    def head_edge(side, later):
        at = jnp.where(side == near, 0, rows + 1)
        which = jnp.where(side < 0, 0, 1) + 2 * later
        return remote(
            part.at[later, at], from_side.at[which], send_head.at[which], recv_head.at[which], (t + later, s + side)
        )

    head_onward = remote(part.at[1, pl.ds(1, rows)], from_time, send_head.at[4], recv_head.at[4], (t + 1, s))

    for side in (near, far):
        for later in range(2):
            sent = exists(side) & older if later else exists(side)

            @pl.when(jnp.logical_not(sent))
            def _():
                from_side[jnp.where(side < 0, 1, 0) + 2 * later] = jnp.zeros((8, width), F32)

    @pl.when(jnp.logical_not(older))
    def _():
        from_time[...] = jnp.zeros((rows, 8, width), F32)

    summed = {}
    lane = lax.broadcasted_iota(jnp.int32, (8, width), 1)

    def settle(place):
        for late in range(2):
            part[late, place] = shifted_sum(*[summed[late, place, c] for c in range(3)], lane)

    def collect(i, product):
        for c in range(3):
            for b in range(3):
                for late in range(2):
                    at = ((c * 3 + b) * 2 + late) * 8
                    piece = product[at : at + 8]
                    key = (late, i + 2 - b, c)
                    summed[key] = summed[key] + piece if key in summed else piece

    waiting = []
    for i in [0, rows - 1, *middle]:
        r = order[i]
        if i in (0, rows - 1):
            await_side(ext_two, sems_two, far if i else near)
        branch = conv_row(taps_two, ext_two, r)
        heads = []
        for f in range(2):
            total = (own[f, r].astype(F32) + branch[f]).astype(BF16).astype(F32)
            heads.append(act(total, gain_head))
        heads = jnp.concatenate(heads, axis=0)
        if i in middle:
            waiting.append(heads)
            if i != middle[-1]:
                continue
            product = jnp.dot(head_weights, jnp.concatenate(waiting, axis=1), preferred_element_type=F32)
            for n, at in enumerate(middle):
                collect(at, product[:, n * width : (n + 1) * width])
            continue
        product = jnp.dot(head_weights, heads, preferred_element_type=F32)
        collect(i, product)
        if i == 0:
            settle(0)
            send_both(head_edge, near, newer & exists(near))
        if i == rows - 1:
            settle(rows + 1)
            send_both(head_edge, far, newer & exists(far))
    for place in range(1, rows + 1):
        settle(place)
    pl.when(newer)(head_onward.start)

    drain(ext_one, sems_one)
    pl.when(lent & above)(handed_on().wait_send)
    drain(ext_two, sems_two)
    pl.when(older)(head_onward.wait_recv)
    for i, r in enumerate(order):
        total = part[0, i + 1] + from_time[i]
        for at, side in ((0, near), (rows - 1, far)):
            if i == at:
                pl.when(exists(side))(head_edge(-side, 0).wait_recv)
                pl.when(older & exists(side))(head_edge(-side, 1).wait_recv)
                came = jnp.where(side < 0, 1, 0)
                total = total + from_side[came] + from_side[came + 2]
        for f in range(2):
            for o in range(3):
                out_ref[f, o, pl.ds(r, 1)] = total[4 * f + o : 4 * f + o + 1]

    for side in (near, far):
        pl.when(exists(side))(head_edge(side, 0).wait_send)
        pl.when(newer & exists(side))(head_edge(side, 1).wait_send)
    pl.when(newer)(head_onward.wait_send)


def local(times, tiles, features, gain_one, gain_two, gain_head, conv_one, conv_two, conv_head):
    frames, rows, chans, width = features.shape
    anywhere = pl.BlockSpec(memory_space=pl.ANY)
    vmem = pl.BlockSpec(memory_space=pltpu.VMEM)
    ext = pltpu.VMEM((4, (rows + 2) * chans, width), BF16)
    raw = pltpu.VMEM((9, 3 * chans, chans), BF16)
    taps = pltpu.VMEM((3 * chans, 9 * chans), BF16)
    dma = pltpu.SemaphoreType.DMA
    decoded = pl.pallas_call(
        functools.partial(kernel, (times, tiles, rows, chans, width)),
        out_shape=jax.ShapeDtypeStruct((frames, 3, rows, width), F32),
        in_specs=[anywhere] * 7,
        out_specs=vmem,
        scratch_shapes=[
            pltpu.VMEM(features.shape, BF16),
            pltpu.VMEM((1, chans), F32),
            pltpu.VMEM((1, chans), F32),
            pltpu.VMEM((1, chans), F32),
            pltpu.VMEM(conv_head.shape, BF16),
            raw,
            raw,
            taps,
            taps,
            pltpu.VMEM((144, 2 * chans), F32),
            ext,
            ext,
            pltpu.VMEM((2, rows + 2, 8, width), F32),
            pltpu.VMEM((rows, 8, width), F32),
            pltpu.VMEM((4, 8, width), F32),
            dma((7,)),
            dma((8,)),
            dma((8,)),
            dma((8,)),
            dma((8,)),
            dma((5,)),
            dma((5,)),
            pltpu.SemaphoreType.REGULAR,
        ],
        compiler_params=pltpu.CompilerParams(
            collective_id=0, has_side_effects=True, vmem_limit_bytes=48 * 1024 * 1024
        ),
        cost_estimate=pl.CostEstimate(flops=1_100_000_000, bytes_accessed=1_300_000, transcendentals=400_000),
        name="decode",
    )(
        *(
            pltpu.with_memory_space_constraint(operand, pltpu.HBM)
            for operand in (
                features,
                gain_one.reshape(1, chans),
                gain_two.reshape(1, chans),
                gain_head.reshape(1, chans),
                conv_one.reshape(9, 3 * chans, chans),
                conv_two.reshape(9, 3 * chans, chans),
                conv_head,
            )
        )
    )
    return jnp.transpose(decoded, (0, 2, 1, 3))


def solution(mesh):
    placed = (P("tm", "tile", None, None), P(), P(), P(), P(), P(), P())
    return jax.shard_map(
        functools.partial(local, mesh.shape["tm"], mesh.shape["tile"]),
        mesh=mesh,
        in_specs=placed,
        out_specs=P("tm", "tile", None, None),
        check_vma=False,
    )
```

```python
import functools

import jax
import jax.numpy as jnp
from jax import lax
from jax.experimental import pallas as pl
from jax.experimental.pallas import tpu as pltpu
from jax.sharding import PartitionSpec as P

MESH = pl.DeviceIdType.MESH
F32 = jnp.float32
BF16 = jnp.bfloat16


def act(values, gains):
    square = jnp.sum(values * values, axis=0, keepdims=True) * (1.0 / values.shape[0])
    half = values * lax.rsqrt(square + 1e-06) * (gains * 0.5)
    return (half * jnp.tanh(half) + half).astype(BF16)


def shifted_sum(left, middle, right, column):
    width = column.shape[1]
    from_left = jnp.where(column == 0, 0.0, pltpu.roll(left, 1, 1))
    from_right = jnp.where(column == width - 1, 0.0, pltpu.roll(right, width - 1, 1))
    return from_left + middle + from_right


def kernel(
    sizes,
    features_ref,
    gain_one_hbm,
    gain_two_hbm,
    gain_head_hbm,
    conv_one_ref,
    conv_two_ref,
    conv_head_hbm,
    out_ref,
    own,
    gain_one_ref,
    gain_two_ref,
    gain_head_ref,
    conv_head_ref,
    raw_one,
    raw_two,
    taps_one,
    taps_two,
    taps_head,
    ext_one,
    ext_two,
    part,
    from_time,
    from_side,
    load_sem,
    send_one,
    recv_one,
    send_two,
    recv_two,
    send_head,
    recv_head,
    ready,
):
    times, tiles, rows, chans, width = sizes
    t, s = lax.axis_index("tm"), lax.axis_index("tile")
    older, newer = t > 0, t < times - 1
    above, below = s > 0, s < tiles - 1

    odd = lax.rem(t, 2) == 1
    even = jnp.logical_not(odd)
    lent = odd & newer & (t == times // 2 - 1)
    lent_to = even & older & (t == times // 2)

    senders = [
        (older & above & jnp.logical_not(lent_to), (-1, -1)),
        (lent & below, (1, 1)),
        (older & below, (-1, 1)),
        (above, (0, -1)),
        (below, (0, 1)),
        (older, (-1, 0)),
    ]
    above_one, below_one, newer_one, lent_one, lent_to_one = (
        flag.astype(jnp.int32) for flag in (above, below, newer, lent, lent_to)
    )
    receivers = above_one + below_one + newer_one * (1 + above_one + below_one)
    receivers = receivers - lent_one * below_one + lent_to_one * above_one
    barrier = pltpu.get_barrier_semaphore()
    for there, (dt, ds) in senders:

        @pl.when(there)
        def _():
            pl.semaphore_signal(barrier, inc=1, device_id=(t + dt, s + ds), device_id_type=MESH)

    loads = [
        pltpu.make_async_copy(source, target, load_sem.at[i])
        for i, (source, target) in enumerate(
            (
                (features_ref, own),
                (gain_one_hbm, gain_one_ref),
                (gain_two_hbm, gain_two_ref),
                (gain_head_hbm, gain_head_ref),
                (conv_one_ref, raw_one),
                (conv_two_ref, raw_two),
                (conv_head_hbm, conv_head_ref),
            )
        )
    ]
    for load in loads:
        load.start()

    for ext in (ext_one, ext_two):

        @pl.when(jnp.logical_not(older))
        def _():
            ext[0:2] = jnp.zeros((2, (rows + 2) * chans, width), BF16)

        @pl.when(jnp.logical_not(above))
        def _():
            ext[:, 0:chans] = jnp.zeros((4, chans, width), BF16)

        @pl.when(jnp.logical_not(below))
        def _():
            ext[:, (rows + 1) * chans :] = jnp.zeros((4, chans, width), BF16)

    upwards = lax.rem(s, 4) < 2
    near, far = jnp.where(upwards, 1, -1), jnp.where(upwards, -1, 1)
    order = [jnp.where(upwards, rows - 1 - i, i) for i in range(rows)]
    middle = list(range(1, rows - 1))

    outer = (lax.rem(s, 4) == 0) | (lax.rem(s, 4) == 3)
    lead = jnp.where(outer & (lax.rem(t, 2) == 0), far, near)
    lead_of_next = jnp.where(outer & (lax.rem(t, 2) == 1), far, near)

    def row_from(side, i):
        return jnp.where(side < 0, i, rows - 1 - i)


    def rows_at(at, count=1):
        return pl.ds(pl.multiple_of(at * chans, 32), count * chans)

    def spread(gain_ref):
        return jnp.transpose(jnp.broadcast_to(gain_ref[...], (width, chans)))

    def exists(side):
        return jnp.where(side < 0, s > 0, s < tiles - 1)

    def remote(source, target, send_sem, recv_sem, device):
        return pltpu.make_async_remote_copy(
            src_ref=source,
            dst_ref=target,
            send_sem=send_sem,
            recv_sem=recv_sem,
            device_id=device,
            device_id_type=MESH,
        )

    def edge(ext, sems, side, later):
        source, target = jnp.where(side < 0, 1, rows), jnp.where(side < 0, rows + 1, 0)
        which = jnp.where(side < 0, 0, 1) + 2 * later
        return remote(
            ext.at[pl.ds(2, 2), rows_at(source)],
            ext.at[pl.ds(2 - 2 * later, 2), rows_at(target)],
            sems[0].at[which],
            sems[1].at[which],
            (t + later, s + side),
        )

    def onward(ext, sems, r):
        return remote(
            ext.at[pl.ds(2, 2), rows_at(r + 1)],
            ext.at[pl.ds(0, 2), rows_at(r + 1)],
            sems[0].at[4 + r],
            sems[1].at[4 + r],
            (t + 1, s),
        )

    def handed_on():
        here = pl.ds(0, chans)
        return remote(
            ext_one.at[pl.ds(2, 2), here], ext_one.at[pl.ds(0, 2), here], send_one.at[3], recv_one.at[3], (t + 1, s)
        )

    def straight(ext, side):
        there = newer & exists(side)
        return there & jnp.logical_not(lent & (side > 0)) if ext is ext_one else there

    def send_both(copy, side, there):
        ahead = odd
        pl.when(there & ahead)(copy(side, 1).start)
        pl.when(exists(side))(copy(side, 0).start)
        pl.when(there & jnp.logical_not(ahead))(copy(side, 1).start)

    def send_edge(ext, sems, side):
        if ext is ext_two:

            @pl.when(lent & below & (side > 0))
            def _():
                pl.semaphore_wait(ready, 1)

        send_both(functools.partial(edge, ext, sems), side, straight(ext, side))

    def send_onward(ext, sems, r):
        pl.when(newer)(onward(ext, sems, r).start)

    def await_edge(ext, sems, side):
        early = lent & (side < 0) if ext is ext_one else t < 0
        pl.when(exists(side) & jnp.logical_not(early))(edge(ext, sems, -side, 0).wait_recv)
        pl.when(older & exists(side))(edge(ext, sems, -side, 1).wait_recv)

    def await_onward(ext, sems, r):
        pl.when(older)(onward(ext, sems, r).wait_recv)

    def await_side(ext, sems, side):
        await_onward(ext, sems, row_from(side, 0))
        await_onward(ext, sems, row_from(side, 1))
        await_edge(ext, sems, side)

    def drain(ext, sems):
        for side in (near, far):
            pl.when(exists(side))(edge(ext, sems, side, 0).wait_send)
            pl.when(straight(ext, side))(edge(ext, sems, side, 1).wait_send)
        for r in order:
            pl.when(newer)(onward(ext, sems, r).wait_send)

    sems_one, sems_two = (send_one, recv_one), (send_two, recv_two)
    column = lax.broadcasted_iota(jnp.int32, (chans, width), 1)

    def first_act(r, gain):
        for f in range(2):
            ext_one[2 + f, rows_at(r + 1)] = act(own[f, r].astype(F32), gain)

    for load in loads[1:4]:
        load.wait()
    gain_one = spread(gain_one_ref)
    loads[0].wait()
    first_act(order[-1], gain_one)
    first_act(order[0], gain_one)
    pl.semaphore_wait(barrier, receivers)

    @pl.when(lent_to & above)
    def _():
        pl.semaphore_signal(ready, inc=1, device_id=(t - 1, s - 1), device_id_type=MESH)

    for side in (far, near):
        send_edge(ext_one, sems_one, side)
    for i in range(rows):
        r = row_from(lead_of_next, i)
        if 0 < i < rows - 1:
            first_act(r, gain_one)
        send_onward(ext_one, sems_one, r)
    gain_two, gain_head = spread(gain_two_ref), spread(gain_head_ref)

    loads[4].wait()
    for k in range(9):
        taps_one[:, k * chans : (k + 1) * chans] = raw_one[k]
    loads[5].wait()
    for k in range(9):
        taps_two[:, k * chans : (k + 1) * chans] = raw_two[k]
    loads[6].wait()
    taps_head[...] = jnp.zeros_like(taps_head)
    for b in range(3):
        step = jnp.where(upwards, 2 - b, b)
        for a in range(3):
            for c in range(3):
                piece = conv_head_ref[a, step, c].astype(F32)
                for f in range(2):
                    target = f + 2 - a
                    at = ((c * 3 + b) * 2 + target // 2) * 8 + (target % 2) * 4
                    taps_head[at : at + 3, f * chans : (f + 1) * chans] = piece
    head_weights = taps_head[...].astype(BF16)

    @pl.when(lent & above)
    def _():
        edge(ext_one, sems_one, 1, 0).wait_recv()
        handed_on().start()

    def conv_row(taps, ext, r):
        stacks = [jnp.concatenate([ext[f + a, rows_at(r, 3)] for a in range(3)], axis=0) for f in range(2)]
        product = jnp.dot(taps[...], jnp.concatenate(stacks, axis=1), preferred_element_type=F32)
        return [
            shifted_sum(
                *[product[c * chans : (c + 1) * chans, f * width : (f + 1) * width] for c in range(3)], column
            )
            for f in range(2)
        ]

    def second_act(r):
        for f, hidden in enumerate(conv_row(taps_one, ext_one, r)):
            hidden = hidden.astype(BF16).astype(F32)
            ext_two[2 + f, rows_at(r + 1)] = act(hidden, gain_two)

    for side in (lead, -lead):
        await_side(ext_one, sems_one, side)
        second_act(row_from(side, 0))
        send_edge(ext_two, sems_two, side)
        send_onward(ext_two, sems_two, row_from(side, 0))
    for i in middle:
        second_act(row_from(lead, i))
        send_onward(ext_two, sems_two, row_from(lead, i))

    def head_edge(side, later):
        at = jnp.where(side == near, 0, rows + 1)
        which = jnp.where(side < 0, 0, 1) + 2 * later
        return remote(
            part.at[later, at], from_side.at[which], send_head.at[which], recv_head.at[which], (t + later, s + side)
        )

    head_onward = remote(part.at[1, pl.ds(1, rows)], from_time, send_head.at[4], recv_head.at[4], (t + 1, s))

    for side in (near, far):
        for later in range(2):
            sent = exists(side) & older if later else exists(side)

            @pl.when(jnp.logical_not(sent))
            def _():
                from_side[jnp.where(side < 0, 1, 0) + 2 * later] = jnp.zeros((8, width), F32)

    @pl.when(jnp.logical_not(older))
    def _():
        from_time[...] = jnp.zeros((rows, 8, width), F32)

    summed = {}
    lane = lax.broadcasted_iota(jnp.int32, (8, width), 1)

    def settle(place):
        for late in range(2):
            part[late, place] = shifted_sum(*[summed[late, place, c] for c in range(3)], lane)

    def collect(i, product):
        for c in range(3):
            for b in range(3):
                for late in range(2):
                    at = ((c * 3 + b) * 2 + late) * 8
                    piece = product[at : at + 8]
                    key = (late, i + 2 - b, c)
                    summed[key] = summed[key] + piece if key in summed else piece

    def heads_of(i):
        r = order[i]
        branch = conv_row(taps_two, ext_two, r)
        heads = []
        for f in range(2):
            total = (own[f, r].astype(F32) + branch[f]).astype(BF16).astype(F32)
            heads.append(act(total, gain_head))
        return jnp.concatenate(heads, axis=0)

    def add_heads(pair, heads):
        product = jnp.dot(head_weights, jnp.concatenate(heads, axis=1), preferred_element_type=F32)
        for n, i in enumerate(pair):
            collect(i, product[:, n * width : (n + 1) * width])

    edges = [0, rows - 1]
    heads = []
    for i in edges:
        await_side(ext_two, sems_two, far if i else near)
        heads.append(heads_of(i))
    add_heads(edges, heads)
    settle(rows + 1)
    send_both(head_edge, far, newer & exists(far))
    settle(0)
    send_both(head_edge, near, newer & exists(near))
    add_heads(middle, [heads_of(i) for i in middle])
    for place in range(1, rows + 1):
        settle(place)
    pl.when(newer)(head_onward.start)

    drain(ext_one, sems_one)
    pl.when(lent & above)(handed_on().wait_send)
    drain(ext_two, sems_two)
    pl.when(older)(head_onward.wait_recv)
    for i, r in enumerate(order):
        total = part[0, i + 1] + from_time[i]
        for at, side in ((0, near), (rows - 1, far)):
            if i == at:
                pl.when(exists(side))(head_edge(-side, 0).wait_recv)
                pl.when(older & exists(side))(head_edge(-side, 1).wait_recv)
                came = jnp.where(side < 0, 1, 0)
                total = total + from_side[came] + from_side[came + 2]
        for f in range(2):
            for o in range(3):
                out_ref[f, o, pl.ds(r, 1)] = total[4 * f + o : 4 * f + o + 1]

    for side in (near, far):
        pl.when(exists(side))(head_edge(side, 0).wait_send)
        pl.when(newer & exists(side))(head_edge(side, 1).wait_send)
    pl.when(newer)(head_onward.wait_send)


def local(times, tiles, features, gain_one, gain_two, gain_head, conv_one, conv_two, conv_head):
    frames, rows, chans, width = features.shape
    anywhere = pl.BlockSpec(memory_space=pl.ANY)
    vmem = pl.BlockSpec(memory_space=pltpu.VMEM)
    ext = pltpu.VMEM((4, (rows + 2) * chans, width), BF16)
    raw = pltpu.VMEM((9, 3 * chans, chans), BF16)
    taps = pltpu.VMEM((3 * chans, 9 * chans), BF16)
    dma = pltpu.SemaphoreType.DMA
    decoded = pl.pallas_call(
        functools.partial(kernel, (times, tiles, rows, chans, width)),
        out_shape=jax.ShapeDtypeStruct((frames, 3, rows, width), F32),
        in_specs=[anywhere] * 7,
        out_specs=vmem,
        scratch_shapes=[
            pltpu.VMEM(features.shape, BF16),
            pltpu.VMEM((1, chans), F32),
            pltpu.VMEM((1, chans), F32),
            pltpu.VMEM((1, chans), F32),
            pltpu.VMEM(conv_head.shape, BF16),
            raw,
            raw,
            taps,
            taps,
            pltpu.VMEM((144, 2 * chans), F32),
            ext,
            ext,
            pltpu.VMEM((2, rows + 2, 8, width), F32),
            pltpu.VMEM((rows, 8, width), F32),
            pltpu.VMEM((4, 8, width), F32),
            dma((7,)),
            dma((8,)),
            dma((8,)),
            dma((8,)),
            dma((8,)),
            dma((5,)),
            dma((5,)),
            pltpu.SemaphoreType.REGULAR,
        ],
        compiler_params=pltpu.CompilerParams(
            collective_id=0, has_side_effects=True, vmem_limit_bytes=48 * 1024 * 1024
        ),
        cost_estimate=pl.CostEstimate(flops=1_100_000_000, bytes_accessed=1_300_000, transcendentals=400_000),
        name="decode",
    )(
        *(
            pltpu.with_memory_space_constraint(operand, pltpu.HBM)
            for operand in (
                features,
                gain_one.reshape(1, chans),
                gain_two.reshape(1, chans),
                gain_head.reshape(1, chans),
                conv_one.reshape(9, 3 * chans, chans),
                conv_two.reshape(9, 3 * chans, chans),
                conv_head,
            )
        )
    )
    return jnp.transpose(decoded, (0, 2, 1, 3))


def solution(mesh):
    placed = (P("tm", "tile", None, None), P(), P(), P(), P(), P(), P())
    return jax.shard_map(
        functools.partial(local, mesh.shape["tm"], mesh.shape["tile"]),
        mesh=mesh,
        in_specs=placed,
        out_specs=P("tm", "tile", None, None),
        check_vma=False,
    )
```

```python
import functools

import jax
import jax.numpy as jnp
from jax import lax
from jax.experimental import pallas as pl
from jax.experimental.pallas import tpu as pltpu
from jax.sharding import PartitionSpec as P

MESH = pl.DeviceIdType.MESH
F32 = jnp.float32
BF16 = jnp.bfloat16


def act(values, gains):
    square = jnp.sum(values * values, axis=0, keepdims=True) * (1.0 / values.shape[0])
    half = values * lax.rsqrt(square + 1e-06) * (gains * 0.5)
    return (half * jnp.tanh(half) + half).astype(BF16)


def shifted_sum(left, middle, right, column):
    width = column.shape[1]
    from_left = jnp.where(column == 0, 0.0, pltpu.roll(left, 1, 1))
    from_right = jnp.where(column == width - 1, 0.0, pltpu.roll(right, width - 1, 1))
    return from_left + middle + from_right


def kernel(
    sizes,
    features_ref,
    gain_one_hbm,
    gain_two_hbm,
    gain_head_hbm,
    conv_one_ref,
    conv_two_ref,
    conv_head_hbm,
    out_ref,
    own,
    gain_one_ref,
    gain_two_ref,
    gain_head_ref,
    conv_head_ref,
    raw_one,
    raw_two,
    taps_one,
    taps_two,
    taps_head,
    ext_one,
    ext_two,
    part,
    from_time,
    from_side,
    load_sem,
    send_one,
    recv_one,
    send_two,
    recv_two,
    send_head,
    recv_head,
    ready,
):
    times, tiles, rows, chans, width = sizes
    t, s = lax.axis_index("tm"), lax.axis_index("tile")
    older, newer = t > 0, t < times - 1
    above, below = s > 0, s < tiles - 1

    odd = lax.rem(t, 2) == 1
    even = jnp.logical_not(odd)
    lent = odd & newer & (t == times // 2 - 1)
    lent_to = even & older & (t == times // 2)

    senders = [
        (older & above & jnp.logical_not(lent_to), (-1, -1)),
        (lent & below, (1, 1)),
        (older & below, (-1, 1)),
        (above, (0, -1)),
        (below, (0, 1)),
        (older, (-1, 0)),
    ]
    above_one, below_one, newer_one, lent_one, lent_to_one = (
        flag.astype(jnp.int32) for flag in (above, below, newer, lent, lent_to)
    )
    receivers = above_one + below_one + newer_one * (1 + above_one + below_one)
    receivers = receivers - lent_one * below_one + lent_to_one * above_one
    barrier = pltpu.get_barrier_semaphore()
    for there, (dt, ds) in senders:

        @pl.when(there)
        def _():
            pl.semaphore_signal(barrier, inc=1, device_id=(t + dt, s + ds), device_id_type=MESH)

    loads = [
        pltpu.make_async_copy(source, target, load_sem.at[i])
        for i, (source, target) in enumerate(
            (
                (features_ref, own),
                (gain_one_hbm, gain_one_ref),
                (gain_two_hbm, gain_two_ref),
                (gain_head_hbm, gain_head_ref),
                (conv_one_ref, raw_one),
                (conv_two_ref, raw_two),
                (conv_head_hbm, conv_head_ref),
            )
        )
    ]
    for load in loads:
        load.start()

    for ext in (ext_one, ext_two):

        @pl.when(jnp.logical_not(older))
        def _():
            ext[0:2] = jnp.zeros((2, (rows + 2) * chans, width), BF16)

        @pl.when(jnp.logical_not(above))
        def _():
            ext[:, 0:chans] = jnp.zeros((4, chans, width), BF16)

        @pl.when(jnp.logical_not(below))
        def _():
            ext[:, (rows + 1) * chans :] = jnp.zeros((4, chans, width), BF16)

    upwards = lax.rem(s, 4) < 2
    near, far = jnp.where(upwards, 1, -1), jnp.where(upwards, -1, 1)
    order = [jnp.where(upwards, rows - 1 - i, i) for i in range(rows)]
    middle = list(range(1, rows - 1))

    outer = (lax.rem(s, 4) == 0) | (lax.rem(s, 4) == 3)
    lead = jnp.where(outer & (lax.rem(t, 2) == 0), far, near)
    lead_of_next = jnp.where(outer & (lax.rem(t, 2) == 1), far, near)

    def row_from(side, i):
        return jnp.where(side < 0, i, rows - 1 - i)


    def rows_at(at, count=1):
        return pl.ds(pl.multiple_of(at * chans, 32), count * chans)

    def spread(gain_ref):
        return jnp.transpose(jnp.broadcast_to(gain_ref[...], (width, chans)))

    def exists(side):
        return jnp.where(side < 0, s > 0, s < tiles - 1)

    def remote(source, target, send_sem, recv_sem, device):
        return pltpu.make_async_remote_copy(
            src_ref=source,
            dst_ref=target,
            send_sem=send_sem,
            recv_sem=recv_sem,
            device_id=device,
            device_id_type=MESH,
        )

    def edge(ext, sems, side, later):
        source, target = jnp.where(side < 0, 1, rows), jnp.where(side < 0, rows + 1, 0)
        which = jnp.where(side < 0, 0, 1) + 2 * later
        return remote(
            ext.at[pl.ds(2, 2), rows_at(source)],
            ext.at[pl.ds(2 - 2 * later, 2), rows_at(target)],
            sems[0].at[which],
            sems[1].at[which],
            (t + later, s + side),
        )

    def onward(ext, sems, r):
        return remote(
            ext.at[pl.ds(2, 2), rows_at(r + 1)],
            ext.at[pl.ds(0, 2), rows_at(r + 1)],
            sems[0].at[4 + r],
            sems[1].at[4 + r],
            (t + 1, s),
        )

    def handed_on():
        here = pl.ds(0, chans)
        return remote(
            ext_one.at[pl.ds(2, 2), here], ext_one.at[pl.ds(0, 2), here], send_one.at[3], recv_one.at[3], (t + 1, s)
        )

    def straight(ext, side):
        there = newer & exists(side)
        return there & jnp.logical_not(lent & (side > 0)) if ext is ext_one else there

    def send_both(copy, side, there, ahead=odd):
        pl.when(there & ahead)(copy(side, 1).start)
        pl.when(exists(side))(copy(side, 0).start)
        pl.when(there & jnp.logical_not(ahead))(copy(side, 1).start)

    def send_edge(ext, sems, side):
        if ext is ext_two:

            @pl.when(lent & below & (side > 0))
            def _():
                pl.semaphore_wait(ready, 1)

        ahead = odd | (t >= times // 2) if ext is ext_one else odd
        send_both(functools.partial(edge, ext, sems), side, straight(ext, side), ahead)

    def send_onward(ext, sems, r):
        pl.when(newer)(onward(ext, sems, r).start)

    def await_edge(ext, sems, side):
        early = lent & (side < 0) if ext is ext_one else t < 0
        pl.when(exists(side) & jnp.logical_not(early))(edge(ext, sems, -side, 0).wait_recv)
        pl.when(older & exists(side))(edge(ext, sems, -side, 1).wait_recv)

    def await_onward(ext, sems, r):
        pl.when(older)(onward(ext, sems, r).wait_recv)

    def await_side(ext, sems, side):
        await_onward(ext, sems, row_from(side, 0))
        await_onward(ext, sems, row_from(side, 1))
        await_edge(ext, sems, side)

    def drain(ext, sems):
        for side in (near, far):
            pl.when(exists(side))(edge(ext, sems, side, 0).wait_send)
            pl.when(straight(ext, side))(edge(ext, sems, side, 1).wait_send)
        for r in order:
            pl.when(newer)(onward(ext, sems, r).wait_send)

    sems_one, sems_two = (send_one, recv_one), (send_two, recv_two)
    column = lax.broadcasted_iota(jnp.int32, (chans, width), 1)

    def first_act(r, gain):
        for f in range(2):
            ext_one[2 + f, rows_at(r + 1)] = act(own[f, r].astype(F32), gain)

    for load in loads[1:4]:
        load.wait()
    gain_one = spread(gain_one_ref)
    loads[0].wait()
    first_act(order[-1], gain_one)
    first_act(order[0], gain_one)
    pl.semaphore_wait(barrier, receivers)

    @pl.when(lent_to & above)
    def _():
        pl.semaphore_signal(ready, inc=1, device_id=(t - 1, s - 1), device_id_type=MESH)

    for side in (far, near):
        send_edge(ext_one, sems_one, side)
    for i in range(rows):
        r = row_from(lead_of_next, i)
        if 0 < i < rows - 1:
            first_act(r, gain_one)
        send_onward(ext_one, sems_one, r)
    gain_two, gain_head = spread(gain_two_ref), spread(gain_head_ref)

    loads[4].wait()
    for k in range(9):
        taps_one[:, k * chans : (k + 1) * chans] = raw_one[k]
    loads[5].wait()
    for k in range(9):
        taps_two[:, k * chans : (k + 1) * chans] = raw_two[k]
    loads[6].wait()
    taps_head[...] = jnp.zeros_like(taps_head)
    for b in range(3):
        step = jnp.where(upwards, 2 - b, b)
        for a in range(3):
            for c in range(3):
                piece = conv_head_ref[a, step, c].astype(F32)
                for f in range(2):
                    target = f + 2 - a
                    at = ((c * 3 + b) * 2 + target // 2) * 8 + (target % 2) * 4
                    taps_head[at : at + 3, f * chans : (f + 1) * chans] = piece
    head_weights = taps_head[...].astype(BF16)

    @pl.when(lent & above)
    def _():
        edge(ext_one, sems_one, 1, 0).wait_recv()
        handed_on().start()

    def conv_row(taps, ext, r):
        stacks = [jnp.concatenate([ext[f + a, rows_at(r, 3)] for a in range(3)], axis=0) for f in range(2)]
        product = jnp.dot(taps[...], jnp.concatenate(stacks, axis=1), preferred_element_type=F32)
        return [
            shifted_sum(
                *[product[c * chans : (c + 1) * chans, f * width : (f + 1) * width] for c in range(3)], column
            )
            for f in range(2)
        ]

    def second_act(r):
        for f, hidden in enumerate(conv_row(taps_one, ext_one, r)):
            hidden = hidden.astype(BF16).astype(F32)
            ext_two[2 + f, rows_at(r + 1)] = act(hidden, gain_two)

    for side in (lead, -lead):
        await_side(ext_one, sems_one, side)
        second_act(row_from(side, 0))
        send_edge(ext_two, sems_two, side)
        send_onward(ext_two, sems_two, row_from(side, 0))
    for i in middle:
        second_act(row_from(lead, i))
        send_onward(ext_two, sems_two, row_from(lead, i))

    def head_edge(side, later):
        at = jnp.where(side == near, 0, rows + 1)
        which = jnp.where(side < 0, 0, 1) + 2 * later
        return remote(
            part.at[later, at], from_side.at[which], send_head.at[which], recv_head.at[which], (t + later, s + side)
        )

    head_onward = remote(part.at[1, pl.ds(1, rows)], from_time, send_head.at[4], recv_head.at[4], (t + 1, s))

    for side in (near, far):
        for later in range(2):
            sent = exists(side) & older if later else exists(side)

            @pl.when(jnp.logical_not(sent))
            def _():
                from_side[jnp.where(side < 0, 1, 0) + 2 * later] = jnp.zeros((8, width), F32)

    @pl.when(jnp.logical_not(older))
    def _():
        from_time[...] = jnp.zeros((rows, 8, width), F32)

    summed = {}
    lane = lax.broadcasted_iota(jnp.int32, (8, width), 1)

    def settle(place):
        for late in range(2):
            part[late, place] = shifted_sum(*[summed[late, place, c] for c in range(3)], lane)

    def collect(i, product):
        for c in range(3):
            for b in range(3):
                for late in range(2):
                    at = ((c * 3 + b) * 2 + late) * 8
                    piece = product[at : at + 8]
                    key = (late, i + 2 - b, c)
                    summed[key] = summed[key] + piece if key in summed else piece

    def heads_of(i):
        r = order[i]
        branch = conv_row(taps_two, ext_two, r)
        heads = []
        for f in range(2):
            total = (own[f, r].astype(F32) + branch[f]).astype(BF16).astype(F32)
            heads.append(act(total, gain_head))
        return jnp.concatenate(heads, axis=0)

    def add_heads(pair, heads):
        product = jnp.dot(head_weights, jnp.concatenate(heads, axis=1), preferred_element_type=F32)
        for n, i in enumerate(pair):
            collect(i, product[:, n * width : (n + 1) * width])

    edges = [0, rows - 1]
    heads = []
    for i in edges:
        await_side(ext_two, sems_two, far if i else near)
        heads.append(heads_of(i))
    add_heads(edges, heads)
    settle(rows + 1)
    send_both(head_edge, far, newer & exists(far))
    settle(0)
    send_both(head_edge, near, newer & exists(near))
    add_heads(middle, [heads_of(i) for i in middle])
    for place in range(1, rows + 1):
        settle(place)
    pl.when(newer)(head_onward.start)

    drain(ext_one, sems_one)
    pl.when(lent & above)(handed_on().wait_send)
    drain(ext_two, sems_two)
    pl.when(older)(head_onward.wait_recv)
    for i, r in enumerate(order):
        total = part[0, i + 1] + from_time[i]
        for at, side in ((0, near), (rows - 1, far)):
            if i == at:
                pl.when(exists(side))(head_edge(-side, 0).wait_recv)
                pl.when(older & exists(side))(head_edge(-side, 1).wait_recv)
                came = jnp.where(side < 0, 1, 0)
                total = total + from_side[came] + from_side[came + 2]
        for f in range(2):
            for o in range(3):
                out_ref[f, o, pl.ds(r, 1)] = total[4 * f + o : 4 * f + o + 1]

    for side in (near, far):
        pl.when(exists(side))(head_edge(side, 0).wait_send)
        pl.when(newer & exists(side))(head_edge(side, 1).wait_send)
    pl.when(newer)(head_onward.wait_send)


def local(times, tiles, features, gain_one, gain_two, gain_head, conv_one, conv_two, conv_head):
    frames, rows, chans, width = features.shape
    anywhere = pl.BlockSpec(memory_space=pl.ANY)
    vmem = pl.BlockSpec(memory_space=pltpu.VMEM)
    ext = pltpu.VMEM((4, (rows + 2) * chans, width), BF16)
    raw = pltpu.VMEM((9, 3 * chans, chans), BF16)
    taps = pltpu.VMEM((3 * chans, 9 * chans), BF16)
    dma = pltpu.SemaphoreType.DMA
    decoded = pl.pallas_call(
        functools.partial(kernel, (times, tiles, rows, chans, width)),
        out_shape=jax.ShapeDtypeStruct((frames, 3, rows, width), F32),
        in_specs=[anywhere] * 7,
        out_specs=vmem,
        scratch_shapes=[
            pltpu.VMEM(features.shape, BF16),
            pltpu.VMEM((1, chans), F32),
            pltpu.VMEM((1, chans), F32),
            pltpu.VMEM((1, chans), F32),
            pltpu.VMEM(conv_head.shape, BF16),
            raw,
            raw,
            taps,
            taps,
            pltpu.VMEM((144, 2 * chans), F32),
            ext,
            ext,
            pltpu.VMEM((2, rows + 2, 8, width), F32),
            pltpu.VMEM((rows, 8, width), F32),
            pltpu.VMEM((4, 8, width), F32),
            dma((7,)),
            dma((8,)),
            dma((8,)),
            dma((8,)),
            dma((8,)),
            dma((5,)),
            dma((5,)),
            pltpu.SemaphoreType.REGULAR,
        ],
        compiler_params=pltpu.CompilerParams(
            collective_id=0, has_side_effects=True, vmem_limit_bytes=48 * 1024 * 1024
        ),
        cost_estimate=pl.CostEstimate(flops=1_100_000_000, bytes_accessed=1_300_000, transcendentals=400_000),
        name="decode",
    )(
        *(
            pltpu.with_memory_space_constraint(operand, pltpu.HBM)
            for operand in (
                features,
                gain_one.reshape(1, chans),
                gain_two.reshape(1, chans),
                gain_head.reshape(1, chans),
                conv_one.reshape(9, 3 * chans, chans),
                conv_two.reshape(9, 3 * chans, chans),
                conv_head,
            )
        )
    )
    return jnp.transpose(decoded, (0, 2, 1, 3))


def solution(mesh):
    placed = (P("tm", "tile", None, None), P(), P(), P(), P(), P(), P())
    return jax.shard_map(
        functools.partial(local, mesh.shape["tm"], mesh.shape["tile"]),
        mesh=mesh,
        in_specs=placed,
        out_specs=P("tm", "tile", None, None),
        check_vma=False,
    )
```
